128 devices in a mesh: region: 4 (over x), blk: 32 (over z, y, core).
Axes of the slice: x: 4, y: 4, z: 4, core: 2. Of those that a mesh axis runs over, the one named last changes fastest.
Arguments:
- node_temp: float32 [1048576], P(('region', 'blk')), may hold values from 0.7 to 1.3
- node_diag: float32 [1048576], P(('region', 'blk')), may hold values from 2 to 8
- node_source: float32 [1048576], P(('region', 'blk')), may hold values from 0.5 to 4
- cond_blocks: bfloat16 [4, 32, 192, 128, 128], P('region', 'blk'), may hold values from 7.772446e-05 to 0.0078125
- cond_rows: int32 [4, 32, 192], P('region', 'blk'), may hold values from 0 to 63
- cond_cols: int32 [4, 32, 192], P('region', 'blk'), may hold values from 0 to 65, as said below
- view_blocks: bfloat16 [4, 32, 96, 256, 256], P('region', 'blk'), may hold values from 1.0371208e-05 to 0.010375977
- view_scales: float32 [4, 32, 96, 4], P('region', 'blk'), may hold values from 0.5 to 2
- view_rows: int32 [4, 32, 96], P('region', 'blk'), may hold values from 0 to 511, as said below
- view_cols: int32 [4, 32, 96], P('region', 'blk'), may hold values from 0 to 63
- band_frac: bfloat16 [2048, 4, 256], P(('region', 'blk')), may hold values from 0.099609375 to 0.5
- absorb: bfloat16 [2048, 4, 256], P(('region', 'blk')), may hold values from 0.29882812 to 1
- emis: bfloat16 [2048, 256], P(('region', 'blk')), may hold values from 0.29882812 to 1
- patch_dest: int32 [2048, 256, 1], P(('region', 'blk')), may hold values from 0 to 127; in each aligned block of 4096 rows (0 to 4095, 4096 to 8191, ..., all dimensions but the last counted through in order) at most 64 rows name the same one
- patch_node: int32 [2048, 256], P(('region', 'blk')), may hold values from 0 to 8191
Outputs:
- node_final: float32 [1048576], P(('region', 'blk'))
- patch_flux: float32 [2048, 256], P(('region', 'blk'))
The draws below stay inside these ranges and needn't reach their ends.
Inputs may be any that keep to these rules, and one draw needn't show every extreme that they name: `patch_dest`: among the patches of one device no device is named more than 64 times, and some device is named exactly 64 times. `cond_cols`: entries 0 and 1 of every device's list are 0 and 65. `view_rows`: among one device's blocks, the rows u with one value of u // 16 hold at most 8 distinct values, and on every device some value of u // 16 has exactly 8.
All inputs are finite; a program needn't handle non-finite values.
Results may differ from the reference program's by a relative error of at most 0.0003.
Values may be sent and summed in bfloat16 or wider, within the bound.
A program may use at most 128 MiB of HBM per device.

```python
import math
import jax
import jax.numpy as jnp
import numpy as np
from jax import lax

VIEW_BLOCK = 256
BANDS = 4
NODE_BLOCK = 128
ITERS = 2
ROW_CAP = 8
PATCH_DEV = 4096
VIEW_DEV = 96
NODE_DEV = 8192
COND_DEV = 192
RB_DEV = 16
VIEW_ROWS = 2048
REGION_ROWS = 512
GROUP_COLS = 64
CAP = 64
NODE_TILES = 64
NODES = 1048576
N_REGION = 4
N_BLK = 32


def draw_cond_cols(key, part):
    key = jax.random.fold_in(key, 7)
    columns = jax.random.randint(key, (N_REGION, N_BLK, COND_DEV), 0, NODE_TILES + 2)
    columns = columns.at[:, :, 0].set(0)
    columns = columns.at[:, :, 1].set(NODE_TILES + 1)
    return columns.astype(jnp.int32)


def draw_view_rows(key, part):
    key = jax.random.fold_in(key, 11)
    key_scores, key_owner, key_slot, key_first = jax.random.split(key, 4)
    scores = jax.random.randint(key_scores, (N_REGION, N_BLK, N_BLK, RB_DEV), 0, 1 << 20)
    scores = scores * RB_DEV + jnp.arange(RB_DEV, dtype=jnp.int32)
    offsets = jnp.argsort(scores, axis=-1)[..., :ROW_CAP].astype(jnp.int32)
    owners = jax.random.randint(key_owner, (N_REGION, N_BLK, VIEW_DEV), 0, N_BLK)
    slots = jax.random.randint(key_slot, (N_REGION, N_BLK, VIEW_DEV), 0, ROW_CAP)
    first = jax.random.randint(key_first, (N_REGION, N_BLK, 1), 0, N_BLK)
    place = jnp.arange(VIEW_DEV, dtype=jnp.int32)[None, None, :]
    owners = jnp.where(place < ROW_CAP, first, owners)
    slots = jnp.where(place < ROW_CAP, place, slots)
    flat = offsets.reshape(N_REGION, N_BLK, N_BLK * ROW_CAP)
    offset = jnp.take_along_axis(flat, owners * ROW_CAP + slots, axis=2)
    return (owners * RB_DEV + offset).astype(jnp.int32)


def with_ends(values, rng, low, high):
    extent = values.shape
    index_at = [jax.random.randint(jax.random.fold_in(rng, axis), (), 0, extent[axis]) for axis in range(len(extent))]
    values = values.at[tuple(index_at)].set(low)
    longest = extent.index(max(extent))
    index_at[longest] = (index_at[longest] + 1) % extent[longest]
    return values.at[tuple(index_at)].set(high)


def block_scale(rng, shape, pieces, smallest, largest):
    level, own = 1.0, jax.random.fold_in(rng, 6)
    for axis_at, blocks in pieces:
        heights = jnp.exp(jax.random.uniform(jax.random.fold_in(own, axis_at), (blocks,), jnp.float32, smallest / len(pieces), largest / len(pieces)))
        level = level * jnp.repeat(heights, shape[axis_at] // blocks).reshape([-1 if axis == axis_at else 1 for axis in range(len(shape))])
    return level


def routed_block(stream_key, own, number, rows, amount, top, limit, lean):
    sequence = jax.random.permutation(stream_key, amount)
    packed, common = load_shares(amount, rows * top, limit, lean, True), load_shares(amount, rows * top, limit, lean, False)
    places = jnp.arange(amount)

    def named(sizes, rotation):
        used = int((sizes > 0).sum())
        fixed = max(1, used // 4)
        passed = fixed + (places - fixed + rotation * (used - fixed)) % max(1, amount - fixed)
        return jnp.zeros((amount,), jnp.int32).at[sequence[jnp.where(places < fixed, places, passed)]].set(jnp.asarray(sizes, jnp.int32))

    sizes = jnp.where(number % 4 == 0, named(packed, number // 4), named(common, number - number // 4 - 1))
    mixed = jax.random.permutation(jax.random.fold_in(own, 3), amount)
    source_of, sink = mixed[0:amount // 2 * 2:2], mixed[1:amount // 2 * 2:2]
    margin = jnp.minimum(sizes[source_of] - 1, limit - sizes[sink]) // 2
    margin = jnp.where((source_of == sequence[0]) | (sink == sequence[0]) | (sizes[sink] == 0), 0, jnp.maximum(margin, 0))
    passed = jax.random.randint(jax.random.fold_in(own, 4), (amount // 2,), 0, 1 << 20) % (margin + 1)
    sizes = sizes.at[source_of].add(-passed).at[sink].add(passed)
    labels = jnp.searchsorted(jnp.cumsum(sizes), jnp.arange(rows * top), side="right").astype(jnp.int32)
    listing = labels.reshape(top, rows).T
    listing = listing[jax.random.permutation(jax.random.fold_in(own, 1), rows)]
    rotation = jax.random.randint(jax.random.fold_in(own, 2), (rows, 1), 0, top)
    return jnp.take_along_axis(listing, (jnp.arange(top)[None, :] + rotation) % top, axis=1)


def load_shares(count, total, reach, slope, full):
    loads = [(1 << 20) // math.isqrt(grade ** slope) + 1 for grade in range(1, count + 1)]
    largest = reach if full else min(reach, max(-(-total // count), total * loads[0] // sum(loads)))
    least = 1 if total - largest >= count - 1 else 0
    counts, spare = [largest] + [least] * (count - 1), total - largest - least * (count - 1)
    while spare > 0:
        movable = [i for i in range(1, count) if counts[i] < largest] or [i for i in range(1, count) if counts[i] < reach]
        whole, remaining = sum([loads[i] for i in movable]), spare
        for i in movable:
            more = min(reach - counts[i], max(1, remaining * loads[i] // whole), spare)
            counts[i] = counts[i] + more
            spare = spare - more
    return np.array(counts)


def setup_inputs(seed: int = 0) -> dict:
    arg_keys = jax.random.split(jax.random.key(seed), 16)
    node_temp = jnp.clip(0.7 + 0.59999996 * jax.random.uniform(arg_keys[0], (NODES,), jnp.float32) ** block_scale(arg_keys[0], (NODES,), ((0, 128),), -0.2, 0.2), 0.7, 1.3)
    node_diag = jnp.clip(jnp.exp(math.log(8.0) - 1.3862944 * jax.random.uniform(arg_keys[1], (NODES,), jnp.float32) ** block_scale(arg_keys[1], (NODES,), ((0, 128),), -0.2, 0.2)), 2.0, 8.0)
    node_source = jnp.clip(0.5 + 3.5 * jax.random.uniform(arg_keys[2], (NODES,), jnp.float32) ** block_scale(arg_keys[2], (NODES,), ((0, 128),), -0.2, 0.2), 0.5, 4.0)
    cond_blocks = jnp.clip(jnp.exp(math.log(0.0078125) - 4.61031033 * jax.random.uniform(arg_keys[3], (N_REGION, N_BLK, COND_DEV, NODE_BLOCK, NODE_BLOCK), jnp.float32) ** block_scale(arg_keys[3], (N_REGION, N_BLK, COND_DEV, NODE_BLOCK, NODE_BLOCK), ((0, 4), (1, 32)), -0.2, 0.2)), 7.772445678710938e-05, 0.0078125).astype(jnp.bfloat16)
    cond_rows = with_ends(jax.random.randint(arg_keys[4], (N_REGION, N_BLK, COND_DEV), 0, NODE_TILES), jax.random.fold_in(arg_keys[4], 1), 0, NODE_TILES - 1).astype(jnp.int32)
    cond_cols = draw_cond_cols(jax.random.fold_in(arg_keys[15], 71), 0)
    view_blocks = jnp.clip(jnp.exp(math.log(0.010375977) - 6.908215 * jax.random.uniform(arg_keys[6], (N_REGION, N_BLK, VIEW_DEV, VIEW_BLOCK, VIEW_BLOCK), jnp.float32) ** block_scale(arg_keys[6], (N_REGION, N_BLK, VIEW_DEV, VIEW_BLOCK, VIEW_BLOCK), ((0, 4), (1, 32)), -0.2, 0.2)), 1.0371208190917969e-05, 0.010375977).astype(jnp.bfloat16)
    view_scales = jnp.clip(jnp.exp(math.log(2.0) - 1.3862944 * jax.random.uniform(arg_keys[7], (N_REGION, N_BLK, VIEW_DEV, BANDS), jnp.float32) ** block_scale(arg_keys[7], (N_REGION, N_BLK, VIEW_DEV, BANDS), ((0, 4), (1, 32)), -0.2, 0.2)), 0.5, 2.0)
    view_rows = draw_view_rows(jax.random.fold_in(arg_keys[15], 71), 0)
    view_cols = with_ends(jax.random.randint(arg_keys[9], (N_REGION, N_BLK, VIEW_DEV), 0, GROUP_COLS), jax.random.fold_in(arg_keys[9], 1), 0, GROUP_COLS - 1).astype(jnp.int32)
    band_frac = jnp.clip(0.099609375 + 0.40039062 * jax.random.uniform(arg_keys[10], (VIEW_ROWS, BANDS, VIEW_BLOCK), jnp.float32) ** block_scale(arg_keys[10], (VIEW_ROWS, BANDS, VIEW_BLOCK), ((0, 128),), -0.2, 0.2), 0.099609375, 0.5).astype(jnp.bfloat16)
    absorb = jnp.clip(0.29882812 + 0.7011719 * jax.random.uniform(arg_keys[11], (VIEW_ROWS, BANDS, VIEW_BLOCK), jnp.float32) ** block_scale(arg_keys[11], (VIEW_ROWS, BANDS, VIEW_BLOCK), ((0, 128),), -0.2, 0.2), 0.29882812, 1.0).astype(jnp.bfloat16)
    emis = jnp.clip(0.29882812 + 0.7011719 * jax.random.uniform(arg_keys[12], (VIEW_ROWS, VIEW_BLOCK), jnp.float32) ** block_scale(arg_keys[12], (VIEW_ROWS, VIEW_BLOCK), ((0, 128),), -0.2, 0.2), 0.29882812, 1.0).astype(jnp.bfloat16)
    patch_dest_keys = jax.random.split(jax.random.fold_in(arg_keys[13], 1), VIEW_ROWS * VIEW_BLOCK // PATCH_DEV)
    patch_dest_turns = jax.random.permutation(jax.random.fold_in(arg_keys[13], 3), VIEW_ROWS * VIEW_BLOCK // PATCH_DEV)
    patch_dest = jax.vmap(lambda own, number: routed_block(jax.random.fold_in(arg_keys[13], 2), own, number, PATCH_DEV, N_REGION * N_BLK, 1, CAP, 2))(patch_dest_keys, patch_dest_turns).reshape((VIEW_ROWS, VIEW_BLOCK, 1))
    patch_node = with_ends(jax.random.randint(arg_keys[14], (VIEW_ROWS, VIEW_BLOCK), 0, NODE_DEV), jax.random.fold_in(arg_keys[14], 1), 0, NODE_DEV - 1).astype(jnp.int32)
    return {"node_temp": node_temp, "node_diag": node_diag, "node_source": node_source, "cond_blocks": cond_blocks, "cond_rows": cond_rows, "cond_cols": cond_cols, "view_blocks": view_blocks, "view_scales": view_scales, "view_rows": view_rows, "view_cols": view_cols, "band_frac": band_frac, "absorb": absorb, "emis": emis, "patch_dest": patch_dest, "patch_node": patch_node}


def radiate(emit, view_blocks, view_scales, view_rows, view_cols):
    device_count = N_REGION * N_BLK
    grouped = emit.reshape(N_REGION, N_BLK, RB_DEV, BANDS, VIEW_BLOCK)

    def visit(carry, inputs):
        blocks, scales, block_rows, block_cols, device = inputs
        region_id = device // N_BLK
        column_id = device % N_BLK
        column_emit = jnp.take(grouped, column_id, axis=1).reshape(GROUP_COLS, BANDS, VIEW_BLOCK)
        col_emit = column_emit[block_cols].astype(jnp.float32)
        products = jnp.einsum("kij,kbj->kbi", blocks.astype(jnp.float32), col_emit)
        products = products * scales[:, :, None]
        partial_value = jax.ops.segment_sum(products, block_rows, num_segments=REGION_ROWS)
        carry = carry.at[region_id].add(partial_value)
        return carry, None

    init = jnp.zeros((N_REGION, REGION_ROWS, BANDS, VIEW_BLOCK), jnp.float32)
    inputs = (view_blocks.reshape(device_count, VIEW_DEV, VIEW_BLOCK, VIEW_BLOCK),
              view_scales.reshape(device_count, VIEW_DEV, BANDS),
              view_rows.reshape(device_count, VIEW_DEV),
              view_cols.reshape(device_count, VIEW_DEV),
              jnp.arange(device_count, dtype=jnp.int32))
    carry, unused = lax.scan(visit, init, inputs)
    return carry.reshape(VIEW_ROWS, BANDS, VIEW_BLOCK)


def conduct(temps, cond_blocks, cond_rows, cond_cols):
    device_count = N_REGION * N_BLK
    tiles = temps.reshape(device_count, NODE_TILES, NODE_BLOCK)
    zero_row = jnp.zeros((1, NODE_BLOCK), temps.dtype)
    before = jnp.concatenate([zero_row, tiles[:-1, -1]], 0)
    after = jnp.concatenate([tiles[1:, 0], zero_row], 0)
    extended = jnp.concatenate([before[:, None], tiles, after[:, None]], 1)

    def apply(inputs):
        blocks, block_rows, block_cols, tile_ext = inputs
        col_temps = tile_ext[block_cols]
        terms = jnp.einsum("kij,kj->ki", blocks.astype(jnp.float32), col_temps,
                           precision=lax.Precision.HIGHEST)
        return jax.ops.segment_sum(terms, block_rows, num_segments=NODE_TILES)

    result = lax.map(apply, (cond_blocks.reshape(device_count, COND_DEV, NODE_BLOCK, NODE_BLOCK),
                             cond_rows.reshape(device_count, COND_DEV),
                             cond_cols.reshape(device_count, COND_DEV),
                             extended))
    return result.reshape(-1)


def reference(node_temp, node_diag, node_source, cond_blocks, cond_rows, cond_cols, view_blocks,
              view_scales, view_rows, view_cols, band_frac, absorb, emis, patch_dest, patch_node):
    destination = patch_dest.reshape(-1).astype(jnp.int32)
    global_node = destination * NODE_DEV + patch_node.reshape(-1).astype(jnp.int32)
    emis_f = emis.astype(jnp.float32)
    emis_sum = jax.ops.segment_sum(emis_f.reshape(-1), global_node, num_segments=NODES)
    temps = node_temp
    patch_flux = jnp.zeros((VIEW_ROWS, VIEW_BLOCK), jnp.float32)
    for iteration in range(ITERS):
        patch_temp = temps[global_node].reshape(VIEW_ROWS, VIEW_BLOCK)
        squared = patch_temp * patch_temp
        quartic = squared * squared
        emit = (band_frac.astype(jnp.float32) * quartic[:, None, :]).astype(jnp.bfloat16)
        irradiance = radiate(emit, view_blocks, view_scales, view_rows, view_cols)
        gained = jnp.sum(absorb.astype(jnp.float32) * irradiance, axis=1)
        patch_flux = gained - emis_f * quartic
        heat = jax.ops.segment_sum(patch_flux.reshape(-1), global_node, num_segments=NODES)
        conducted = conduct(temps, cond_blocks, cond_rows, cond_cols)
        residual = node_diag * temps - conducted - heat - node_source
        magnitude = jnp.abs(temps)
        temps = temps - residual / (node_diag + 4.0 * magnitude * magnitude * magnitude * emis_sum)
    return temps, patch_flux
```

```python
import functools

import jax
import jax.numpy as jnp
from jax import lax
from jax.experimental import pallas as pl
from jax.experimental.pallas import tpu as pltpu
from jax.sharding import PartitionSpec as P

ITERS = 2
REGIONS = 4
COLUMNS = 32
PEERS = REGIONS * COLUMNS
BANDS = 4
RB = 16
VIEW = 256
VIEWS = 96
KPAD = 128
GROUP = RB * REGIONS
SLOTS = 8
CAP = 64
TILES = 64
TILE = 128
CONDS = 192
CPAD = 256
MESH = pl.DeviceIdType.MESH
F32 = jnp.float32
BF16 = jnp.bfloat16
I32 = jnp.int32


def mm(a, b):
    return jnp.dot(a, b, preferred_element_type=F32)


def mm_nt(a, b):
    return lax.dot_general(a, b, (((1,), (1,)), ((), ())), preferred_element_type=F32)


def mm_tn(a, b):
    return lax.dot_general(a, b, (((0,), (0,)), ((), ())), preferred_element_type=F32)


def iota(shape, dim):
    return lax.broadcasted_iota(I32, shape, dim)


def pick(mask):
    return jnp.where(mask, 1.0, 0.0).astype(BF16)


def halves(x):
    upper = x.astype(BF16)
    return upper, (x - upper.astype(F32)).astype(BF16)


def rows_to_slots(left, swap):
    low = iota((COLUMNS, 128), 1) < CAP
    part = [left[i * COLUMNS : (i + 1) * COLUMNS] for i in range(REGIONS)]
    pairs = []
    for i in range(0, REGIONS, 2):
        first, second = part[i], part[i + 1]
        if swap:
            first = pltpu.roll(first, CAP, 1)
        else:
            second = pltpu.roll(second, CAP, 1)
        pairs.append(jnp.where(low, first, second))
    return jnp.concatenate(pairs, axis=1)


def kernel(
    temp_ref,
    diag_ref,
    source_ref,
    crow_ref,
    ccol_ref,
    scale_ref,
    vrow_ref,
    vcol_ref,
    frac_ref,
    absorb_ref,
    emis_ref,
    dest_ref,
    node_ref,
    cond_hbm,
    view_hbm,
    node_out,
    flux_out,
    cb,
    vb,
    ohd,
    ohlo,
    code_mine,
    code_all,
    frac_mine,
    frac_all,
    req_send,
    req_recv,
    ans_send,
    ans_recv,
    ab_send,
    ab_recv,
    g_send,
    g_recv,
    f_send,
    f_recv,
    halo_send,
    halo_recv,
    temps,
    emf,
    hi4,
    lo4,
    em4,
    fh4,
    fl4,
    patchq,
    ftl,
    ecol,
    prod,
    abk,
    ohslot,
    colt,
    terms,
    esum,
    pads,
    scalep,
    load_sem,
    setup_send,
    setup_recv,
    ans_ssem,
    ans_rsem,
    g_ssem,
    g_rsem,
    f_ssem,
    f_rsem,
    halo_ssem,
    halo_rsem,
):
    r = lax.axis_index("region")
    c = lax.axis_index("blk")
    me = r * COLUMNS + c

    def peer(i):
        p = jnp.bitwise_xor(me, i)
        return p, (lax.shift_right_logical(p, 5), jnp.bitwise_and(p, COLUMNS - 1))

    def push(src, dst, ssem, rsem, where):
        pltpu.make_async_remote_copy(
            src_ref=src,
            dst_ref=dst,
            send_sem=ssem,
            recv_sem=rsem,
            device_id=where,
            device_id_type=MESH,
        ).start()

    def drain(ref, sem):
        pltpu.make_async_copy(ref, ref, sem).wait()

    cond_load = pltpu.make_async_copy(cond_hbm, cb, load_sem.at[0])
    view_load = pltpu.make_async_copy(view_hbm, vb, load_sem.at[1])
    cond_load.start()
    view_load.start()

    barrier = pltpu.get_barrier_semaphore()

    def greet(i, carry):
        pl.semaphore_signal(barrier, inc=1, device_id=peer(i)[1], device_id_type=MESH)
        return carry

    lax.fori_loop(1, PEERS, greet, 0)

    temps[...] = temp_ref[...]
    emf[...] = emis_ref[...].astype(F32)
    upper_tri = pick(iota((VIEW, VIEW), 0) < iota((VIEW, VIEW), 1))
    peer_row = iota((PEERS, VIEW), 0)
    slot_row = iota((2 * CAP, VIEW), 0)
    slot_rank = jnp.bitwise_and(slot_row, CAP - 1)
    slot_low = slot_row < CAP

    def route(u, carry):
        count, first, second = carry
        dest = dest_ref[pl.ds(u, 1), :]
        node = node_ref[pl.ds(u, 1), :]
        hit = jnp.where(peer_row == dest, 1.0, 0.0)
        hit16 = hit.astype(BF16)
        before = mm(hit16, upper_tri)
        rank = jnp.sum(hit * (before + count), axis=0, keepdims=True).astype(I32)
        code_mine[pl.ds(u, 1), :] = dest * CAP + rank
        high = (lax.shift_right_logical(node, 7) + 1).astype(F32)
        low = jnp.bitwise_and(node, TILE - 1).astype(F32)
        match = slot_rank == rank
        one = jnp.where(match, jnp.where(slot_low, high, emf[pl.ds(u, 1), :]), 0.0)
        two = jnp.where(match & slot_low, low, 0.0)
        first = first + mm_nt(hit16, one.astype(BF16))
        second = second + mm_nt(hit16, two.astype(BF16))
        count = count + hit[:, VIEW - 1 :] + before[:, VIEW - 1 :]
        return count, first, second

    zero_rows = jnp.zeros((PEERS, 2 * CAP), F32)
    _, first, second = lax.fori_loop(
        0, RB, route, (jnp.zeros((PEERS, 1), F32), zero_rows, zero_rows), unroll=2
    )
    lane_low = iota((PEERS, 2 * CAP), 1) < CAP
    req_send[:, 0, :] = first * jnp.where(lane_low, 128.0, 1.0) + second
    req_send[:, 1, :] = zero_rows

    pads[...] = jnp.full((8, CPAD), -1, I32)
    pads[0:1, 0:VIEWS] = vrow_ref[...]
    pads[1:2, 0:VIEWS] = vcol_ref[...]
    pads[2:3, 0:CONDS] = crow_ref[...]
    pads[3:4, 0:CONDS] = ccol_ref[...]
    vrow = pads[0:1, 0:KPAD]
    vcol = pads[1:2, 0:KPAD]
    crow = pads[2:3, :]
    ccol = pads[3:4, :]
    owner = lax.shift_right_arithmetic(vrow, 4)
    offset = jnp.bitwise_and(vrow, RB - 1)
    owner_hit = pick(iota((COLUMNS, KPAD), 0) == owner)
    offset_hit = jnp.where(iota((128, KPAD), 0) == offset, 1.0, 0.0)
    present = jnp.where(mm_nt(owner_hit, offset_hit.astype(BF16)) > 0.5, 1.0, 0.0)
    tri128 = pick(iota((128, 128), 0) < iota((128, 128), 1))
    place = mm(present.astype(BF16), tri128)
    place_of = mm_tn(place.astype(BF16), owner_hit)
    slot = owner * SLOTS + jnp.sum(offset_hit * place_of, axis=0, keepdims=True).astype(I32)
    ohslot[...] = pick(iota((COLUMNS * SLOTS, KPAD), 0) == slot)
    slot_lane = iota((COLUMNS, 128), 1)
    lane_slot = jnp.bitwise_and(slot_lane, SLOTS - 1).astype(F32)
    table = jnp.zeros((COLUMNS, 128), F32)
    for f in range(RB):
        held = jnp.where(present[:, f : f + 1] > 0.5, place[:, f : f + 1], -1.0)
        table = table + jnp.where(lane_slot == held, f + 1.0, 0.0)
    own_lanes = lax.shift_right_logical(slot_lane, 3) == jnp.bitwise_and(c, 15)
    req_send[pl.ds(r * COLUMNS, COLUMNS), 1, :] = jnp.where(own_lanes, table, 0.0)

    for b in range(BANDS):
        frac_mine[b] = frac_ref[:, b, :]
    ohcol = pick(iota((GROUP, KPAD), 0) == vcol)
    scalep[...] = jnp.zeros((KPAD, BANDS), F32)
    scalep[0:VIEWS, :] = scale_ref[...]
    terms[...] = jnp.zeros((CPAD, TILE), F32)
    oh_ctile = pick(iota((TILES, CPAD), 0) == crow)
    ccol_at = jnp.where(ccol == 0, TILES, jnp.where(ccol == TILES + 1, TILES + 1, ccol - 1))
    oh_ccol = pick(iota((TILES + 16, CPAD), 0) == jnp.where(ccol < 0, -1, ccol_at))

    pl.semaphore_wait(barrier, PEERS - 1)

    def send_request(i, carry):
        p, where = peer(i)
        push(req_send.at[p], req_recv.at[me], setup_send.at[0], setup_recv.at[0], where)
        return carry

    lax.fori_loop(1, PEERS, send_request, 0)
    req_recv[pl.ds(me, 1)] = req_send[pl.ds(me, 1)]
    mine = pl.ds(pl.multiple_of(r * RB, RB), RB)
    for i in range(1, REGIONS):
        where = (jnp.bitwise_xor(r, i), c)
        push(code_mine, code_all.at[mine], setup_send.at[1], setup_recv.at[1], where)
        push(frac_mine, frac_all.at[:, mine, :], setup_send.at[2], setup_recv.at[2], where)
    code_all[mine, :] = code_mine[...]
    frac_all[:, mine, :] = frac_mine[...]

    after = lax.rem(me + 1, PEERS)
    ahead = lax.rem(me + PEERS - 1, PEERS)
    after_id = (lax.shift_right_logical(after, 5), jnp.bitwise_and(after, COLUMNS - 1))
    ahead_id = (lax.shift_right_logical(ahead, 5), jnp.bitwise_and(ahead, COLUMNS - 1))

    def send_halo(it):
        halo_send[it, 0] = temps[TILES - 1 :, :]
        halo_send[it, 1] = temps[0:1, :]
        push(
            halo_send.at[it, 0], halo_recv.at[it, 0], halo_ssem.at[it, 0], halo_rsem.at[it, 0], after_id
        )
        push(
            halo_send.at[it, 1], halo_recv.at[it, 1], halo_ssem.at[it, 1], halo_rsem.at[it, 1], ahead_id
        )

    def wait_halo(it):
        for s in range(2):
            drain(halo_recv.at[it, s], halo_rsem.at[it, s])
            drain(halo_send.at[it, s], halo_ssem.at[it, s])

    send_halo(0)

    others = pl.ds(0, (REGIONS - 1) * RB)
    drain(code_all.at[others], setup_recv.at[1])
    drain(code_all.at[others], setup_send.at[1])

    def build_dest(q, carry):
        ohd[q] = pick(peer_row == lax.shift_right_logical(code_all[pl.ds(q, 1), :], 6))
        return carry

    lax.fori_loop(0, GROUP, build_dest, 0, unroll=4)
    drain(frac_all.at[:, others, :], setup_recv.at[2])
    drain(frac_all.at[:, others, :], setup_send.at[2])

    drain(req_recv.at[0 : PEERS - 1], setup_recv.at[0])
    drain(req_recv.at[0 : PEERS - 1], setup_send.at[0])
    asked = req_recv[:, 0, :]
    code4 = rows_to_slots(asked, False).astype(I32)
    em4[...] = rows_to_slots(asked, True)
    hi4[...] = lax.shift_right_logical(code4, 7) - 1
    lo4[...] = jnp.bitwise_and(code4, TILE - 1)
    tile_row = iota((TILES, VIEW), 0)
    node_row = iota((TILE, VIEW), 0)

    def build_node(j, carry):
        ohlo[j] = pick(node_row == lo4[pl.ds(j, 1), :])
        return carry

    lax.fori_loop(0, COLUMNS, build_node, 0, unroll=4)

    def answer(it):
        up, down = halves(temps[...])
        both = jnp.concatenate([up, down], axis=0)

        def look(j, carry):
            found = mm(both, ohlo[j])
            found = found[0:TILES] + found[TILES:]
            ans_send[j] = jnp.sum(
                jnp.where(tile_row == hi4[pl.ds(j, 1), :], found, 0.0), axis=0, keepdims=True
            )
            return carry

        lax.fori_loop(0, COLUMNS, look, 0, unroll=8)

        def send(i, carry):
            p, where = peer(i)
            push(ans_send.at[where[1]], ans_recv.at[it, me], ans_ssem.at[it], ans_rsem.at[it], where)
            return carry

        lax.fori_loop(1, PEERS, send, 0)
        ans_recv[it, pl.ds(me, 1)] = ans_send[pl.ds(c, 1)]

    def conduct(it):
        wait_halo(it)
        before = jnp.where(me == 0, 0.0, halo_recv[it, 0])
        behind = jnp.where(me == PEERS - 1, 0.0, halo_recv[it, 1])
        edge_row = iota((16, TILE), 0)
        edges = jnp.where(edge_row == 0, before, jnp.where(edge_row == 1, behind, 0.0))
        up, down = halves(jnp.concatenate([temps[...], edges], axis=0))
        colt[...] = mm_tn(oh_ccol, jnp.concatenate([up, down], axis=1))
        eight = iota((8, TILE), 0)

        def group(g, carry):
            rows = colt[pl.ds(pl.multiple_of(g * 8, 8), 8), :]
            left = jnp.concatenate([rows[:, 0:TILE], rows[:, TILE:]], axis=0).astype(BF16)
            total = jnp.zeros((8, TILE), F32)
            for a in range(8):
                part = mm_nt(left, cb[g * 8 + a])
                total = jnp.where(eight == a, part[0:8] + part[8:16], total)
            terms[pl.ds(pl.multiple_of(g * 8, 8), 8), :] = total
            return carry

        lax.fori_loop(0, CONDS // 8, group, 0)
        up, down = halves(terms[...])
        return mm(oh_ctile, up) + mm(oh_ctile, down)

    answer(0)

    codes = req_recv[pl.ds(r * COLUMNS, COLUMNS), 1, :]
    row_codes = jnp.concatenate(
        [
            jnp.sum(codes[0:16], axis=0, keepdims=True),
            jnp.sum(codes[16:32], axis=0, keepdims=True),
        ],
        axis=1,
    ).astype(I32)
    ohrow = pick(iota((RB, COLUMNS * SLOTS), 0) + 1 == row_codes)
    for b in range(0, BANDS, 2):
        pair = [
            mm_tn(ohrow, absorb_ref[:, b + i, :]).reshape(COLUMNS, SLOTS, VIEW) for i in range(2)
        ]
        ab_send[:, b * SLOTS : (b + 2) * SLOTS, :] = jnp.concatenate(pair, axis=1).astype(BF16)

    def send_absorb(i, carry):
        p = jnp.bitwise_xor(c, i)
        push(ab_send.at[p], ab_recv.at[c], setup_send.at[3], setup_recv.at[3], (r, p))
        return carry

    lax.fori_loop(1, COLUMNS, send_absorb, 0)
    ab_recv[pl.ds(c, 1)] = ab_send[pl.ds(c, 1)]

    def gather_emis(j, acc):
        spread = jnp.where(tile_row == hi4[pl.ds(j, 1), :], em4[pl.ds(j, 1), :], 0.0)
        return acc + mm_nt(spread.astype(BF16), ohlo[j])

    esum[...] = lax.fori_loop(0, COLUMNS, gather_emis, jnp.zeros((TILES, TILE), F32), unroll=4)

    rank_row = iota((CAP, VIEW), 0)

    for it in range(ITERS):
        if it > 0:
            answer(it)
        drain(ans_recv.at[it, 0 : PEERS - 1], ans_rsem.at[it])
        drain(ans_recv.at[it, 0 : PEERS - 1], ans_ssem.at[it])
        up, down = halves(ans_recv[it, :, 0, :].T)
        for i in range(REGIONS):
            span = slice(i * CAP, (i + 1) * CAP)
            ftl[i] = jnp.concatenate([up[span], down[span]], axis=0)

        def unpack(q, carry):
            found = mm(ftl[lax.shift_right_logical(q, 4)], ohd[q])
            found = found[0:CAP] + found[CAP:]
            rank = jnp.bitwise_and(code_all[pl.ds(q, 1), :], CAP - 1)
            value = jnp.sum(jnp.where(rank_row == rank, found, 0.0), axis=0, keepdims=True)
            squared = value * value
            patchq[pl.ds(q, 1), :] = squared * squared
            return carry

        lax.fori_loop(0, GROUP, unpack, 0, unroll=8)
        quartic = patchq[...]
        for b in range(BANDS):
            emit = (frac_all[b].astype(F32) * quartic).astype(BF16)
            ecol[b] = mm_tn(ohcol, emit)
        if it == 0:
            view_load.wait()

        def view(k, carry):
            prod[:, k, :] = mm_nt(ecol[:, k, :].astype(BF16), vb[k])
            return carry

        lax.fori_loop(0, VIEWS, view, 0, unroll=8)
        if it == 0:
            drain(ab_recv.at[0 : COLUMNS - 1], setup_recv.at[3])
            drain(ab_recv.at[0 : COLUMNS - 1], setup_send.at[3])
            rows = ab_recv[...].astype(F32)
            for b in range(BANDS):
                mine_b = rows[:, b * SLOTS : (b + 1) * SLOTS, :].reshape(COLUMNS * SLOTS, VIEW)
                abk[b] = mm_tn(ohslot[...], mine_b.astype(BF16)) * scalep[:, b : b + 1]
        gained = prod[0] * abk[0, 0:VIEWS]
        for b in range(1, BANDS):
            gained = gained + prod[b] * abk[b, 0:VIEWS]
        up, down = halves(
            jnp.concatenate([gained, jnp.zeros((KPAD - VIEWS, VIEW), F32)], axis=0)
        )
        g_send[...] = (mm(ohslot[...], up) + mm(ohslot[...], down)).reshape(COLUMNS, SLOTS, VIEW)

        def send_rows(i, carry):
            p = jnp.bitwise_xor(c, i)
            push(g_send.at[p], g_recv.at[it, c], g_ssem.at[it], g_rsem.at[it], (r, p))
            return carry

        lax.fori_loop(1, COLUMNS, send_rows, 0)
        g_recv[it, pl.ds(c, 1)] = g_send[pl.ds(c, 1)]
        if it == 0:
            cond_load.wait()
        conducted = conduct(it)
        drain(g_recv.at[it, 0 : COLUMNS - 1], g_rsem.at[it])
        drain(g_recv.at[it, 0 : COLUMNS - 1], g_ssem.at[it])
        up, down = halves(g_recv[it].reshape(COLUMNS * SLOTS, VIEW))
        flux = mm(ohrow, up) + mm(ohrow, down) - emf[...] * patchq[mine, :]
        flux_out[...] = flux
        up, down = halves(flux)
        up, down = up.astype(F32), down.astype(F32)
        packed = jnp.zeros((PEERS, 2 * CAP), F32)
        for u in range(RB):
            rank = jnp.bitwise_and(code_mine[u : u + 1, :], CAP - 1)
            spread = jnp.where(
                slot_rank == rank, jnp.where(slot_low, up[u : u + 1], down[u : u + 1]), 0.0
            )
            packed = packed + mm_nt(ohd[r * RB + u], spread.astype(BF16))
        f_send[:, 0, :] = packed

        def send_flux(i, carry):
            p, where = peer(i)
            push(f_send.at[p], f_recv.at[it, me], f_ssem.at[it], f_rsem.at[it], where)
            return carry

        lax.fori_loop(1, PEERS, send_flux, 0)
        f_recv[it, pl.ds(me, 1)] = f_send[pl.ds(me, 1)]
        drain(f_recv.at[it, 0 : PEERS - 1], f_rsem.at[it])
        drain(f_recv.at[it, 0 : PEERS - 1], f_ssem.at[it])
        came = f_recv[it, :, 0, :]
        fh4[...] = rows_to_slots(came, False)
        fl4[...] = rows_to_slots(came, True)

        def gather_heat(j, acc):
            hit = tile_row == hi4[pl.ds(j, 1), :]
            spread = jnp.concatenate(
                [
                    jnp.where(hit, fh4[pl.ds(j, 1), :], 0.0).astype(BF16),
                    jnp.where(hit, fl4[pl.ds(j, 1), :], 0.0).astype(BF16),
                ],
                axis=0,
            )
            return acc + mm_nt(spread, ohlo[j])

        heat = lax.fori_loop(
            0, COLUMNS, gather_heat, jnp.zeros((2 * TILES, TILE), F32), unroll=4
        )
        old = temps[...]
        residual = (
            diag_ref[...] * old - conducted - (heat[0:TILES] + heat[TILES:]) - source_ref[...]
        )
        magnitude = jnp.abs(old)
        new = old - residual / (
            diag_ref[...] + 4.0 * magnitude * magnitude * magnitude * esum[...]
        )
        if it + 1 < ITERS:
            temps[...] = new
            send_halo(it + 1)
        else:
            node_out[...] = new


def shards(
    node_temp,
    node_diag,
    node_source,
    cond_blocks,
    cond_rows,
    cond_cols,
    view_blocks,
    view_scales,
    view_rows,
    view_cols,
    band_frac,
    absorb,
    emis,
    patch_dest,
    patch_node,
):
    vmem = pl.BlockSpec(memory_space=pltpu.VMEM)
    hbm = pl.BlockSpec(memory_space=pl.ANY)
    dma = pltpu.SemaphoreType.DMA
    node_final, patch_flux = pl.pallas_call(
        kernel,
        out_shape=(
            jax.ShapeDtypeStruct((TILES, TILE), F32),
            jax.ShapeDtypeStruct((RB, VIEW), F32),
        ),
        in_specs=[vmem] * 13 + [hbm] * 2,
        out_specs=(vmem, vmem),
        scratch_shapes=[
            pltpu.VMEM((CONDS, TILE, TILE), BF16),
            pltpu.VMEM((VIEWS, VIEW, VIEW), BF16),
            pltpu.VMEM((GROUP, PEERS, VIEW), BF16),
            pltpu.VMEM((COLUMNS, TILE, VIEW), BF16),
            pltpu.VMEM((RB, VIEW), I32),
            pltpu.VMEM((GROUP, VIEW), I32),
            pltpu.VMEM((BANDS, RB, VIEW), BF16),
            pltpu.VMEM((BANDS, GROUP, VIEW), BF16),
            pltpu.VMEM((PEERS, 2, 2 * CAP), F32),
            pltpu.VMEM((PEERS, 2, 2 * CAP), F32),
            pltpu.VMEM((COLUMNS, 1, REGIONS * CAP), F32),
            pltpu.VMEM((ITERS, PEERS, 1, REGIONS * CAP), F32),
            pltpu.VMEM((COLUMNS, BANDS * SLOTS, VIEW), BF16),
            pltpu.VMEM((COLUMNS, BANDS * SLOTS, VIEW), BF16),
            pltpu.VMEM((COLUMNS, SLOTS, VIEW), F32),
            pltpu.VMEM((ITERS, COLUMNS, SLOTS, VIEW), F32),
            pltpu.VMEM((PEERS, 1, 2 * CAP), F32),
            pltpu.VMEM((ITERS, PEERS, 1, 2 * CAP), F32),
            pltpu.VMEM((ITERS, 2, 1, TILE), F32),
            pltpu.VMEM((ITERS, 2, 1, TILE), F32),
            pltpu.VMEM((TILES, TILE), F32),
            pltpu.VMEM((RB, VIEW), F32),
            pltpu.VMEM((COLUMNS, REGIONS * CAP), I32),
            pltpu.VMEM((COLUMNS, REGIONS * CAP), I32),
            pltpu.VMEM((COLUMNS, REGIONS * CAP), F32),
            pltpu.VMEM((COLUMNS, REGIONS * CAP), F32),
            pltpu.VMEM((COLUMNS, REGIONS * CAP), F32),
            pltpu.VMEM((GROUP, VIEW), F32),
            pltpu.VMEM((REGIONS, 2 * CAP, PEERS), BF16),
            pltpu.VMEM((BANDS, KPAD, VIEW), F32),
            pltpu.VMEM((BANDS, VIEWS, VIEW), F32),
            pltpu.VMEM((BANDS, KPAD, VIEW), F32),
            pltpu.VMEM((COLUMNS * SLOTS, KPAD), BF16),
            pltpu.VMEM((CPAD, 2 * TILE), F32),
            pltpu.VMEM((CPAD, TILE), F32),
            pltpu.VMEM((TILES, TILE), F32),
            pltpu.VMEM((8, CPAD), I32),
            pltpu.VMEM((KPAD, BANDS), F32),
            dma((2,)),
            dma((4,)),
            dma((4,)),
            dma((ITERS,)),
            dma((ITERS,)),
            dma((ITERS,)),
            dma((ITERS,)),
            dma((ITERS,)),
            dma((ITERS,)),
            dma((ITERS, 2)),
            dma((ITERS, 2)),
        ],
        compiler_params=pltpu.CompilerParams(
            collective_id=0, has_side_effects=True, vmem_limit_bytes=48 * 1024 * 1024
        ),
    )(
        node_temp.reshape(TILES, TILE),
        node_diag.reshape(TILES, TILE),
        node_source.reshape(TILES, TILE),
        cond_rows.reshape(1, CONDS),
        cond_cols.reshape(1, CONDS),
        view_scales.reshape(VIEWS, BANDS),
        view_rows.reshape(1, VIEWS),
        view_cols.reshape(1, VIEWS),
        band_frac,
        absorb,
        emis,
        patch_dest.reshape(RB, VIEW),
        patch_node,
        cond_blocks.reshape(CONDS, TILE, TILE),
        view_blocks.reshape(VIEWS, VIEW, VIEW),
    )
    return node_final.reshape(TILES * TILE), patch_flux


def solution(mesh):
    placed = (
        P(("region", "blk")),
        P(("region", "blk")),
        P(("region", "blk")),
        P("region", "blk", None, None, None),
        P("region", "blk", None),
        P("region", "blk", None),
        P("region", "blk", None, None, None),
        P("region", "blk", None, None),
        P("region", "blk", None),
        P("region", "blk", None),
        P(("region", "blk"), None, None),
        P(("region", "blk"), None, None),
        P(("region", "blk"), None),
        P(("region", "blk"), None, None),
        P(("region", "blk"), None),
    )
    return jax.shard_map(
        shards,
        mesh=mesh,
        in_specs=placed,
        out_specs=(P(("region", "blk")), P(("region", "blk"), None)),
        check_vma=False,
    )
```

```python
import functools

import jax
import jax.numpy as jnp
from jax import lax
from jax.experimental import pallas as pl
from jax.experimental.pallas import tpu as pltpu
from jax.sharding import PartitionSpec as P

ITERS = 2
REGIONS = 4
COLUMNS = 32
PEERS = REGIONS * COLUMNS
BANDS = 4
RB = 16
VIEW = 256
VIEWS = 96
KPAD = 128
GROUP = RB * REGIONS
SLOTS = 8
CAP = 64
TILES = 64
TILE = 128
CONDS = 192
CPAD = 256
MESH = pl.DeviceIdType.MESH
F32 = jnp.float32
BF16 = jnp.bfloat16
I32 = jnp.int32


FAR_GROUPS = [
    rx * 32 + z * 8
    for rx, z in sorted(
        ((rx, z) for rx in range(4) for z in range(4)),
        key=lambda g: -((0, 1, 2, 1)[g[0]] + (0, 1, 2, 1)[g[1]]),
    )
]


def mm(a, b):
    return jnp.dot(a, b, preferred_element_type=F32)


def mm_nt(a, b):
    return lax.dot_general(a, b, (((1,), (1,)), ((), ())), preferred_element_type=F32)


def mm_tn(a, b):
    return lax.dot_general(a, b, (((0,), (0,)), ((), ())), preferred_element_type=F32)


def iota(shape, dim):
    return lax.broadcasted_iota(I32, shape, dim)


def pick(mask):
    return jnp.where(mask, 1.0, 0.0).astype(BF16)


def halves(x):
    upper = x.astype(BF16)
    return upper, (x - upper.astype(F32)).astype(BF16)


def rows_to_slots(left, swap):
    low = iota((COLUMNS, 128), 1) < CAP
    part = [left[i * COLUMNS : (i + 1) * COLUMNS] for i in range(REGIONS)]
    pairs = []
    for i in range(0, REGIONS, 2):
        first, second = part[i], part[i + 1]
        if swap:
            first = pltpu.roll(first, CAP, 1)
        else:
            second = pltpu.roll(second, CAP, 1)
        pairs.append(jnp.where(low, first, second))
    return jnp.concatenate(pairs, axis=1)


def kernel(
    dest_hbm,
    node_hbm,
    emis_hbm,
    temp_hbm,
    vrow_hbm,
    vcol_hbm,
    frac_hbm,
    crow_hbm,
    ccol_hbm,
    scale_hbm,
    absorb_hbm,
    diag_hbm,
    source_hbm,
    cond_hbm,
    view_hbm,
    node_out,
    flux_out,
    dest_ref,
    node_ref,
    emis_ref,
    temps,
    vrow_ref,
    vcol_ref,
    frac_ref,
    crow_ref,
    ccol_ref,
    scale_ref,
    absorb_ref,
    diag_ref,
    source_ref,
    cb,
    vb,
    ohd,
    ohlo,
    code_mine,
    code_all,
    frac_mine,
    frac_all,
    req_send,
    req_recv,
    ans_send,
    ans_recv,
    ab_send,
    ab_recv,
    g_send,
    g_recv,
    f_send,
    f_recv,
    halo_send,
    halo_recv,
    emf,
    hi4,
    lo4,
    em4,
    fh4,
    fl4,
    patchq,
    ftl,
    ecol,
    prod,
    abk,
    ohslot,
    colt,
    terms,
    esum,
    pads,
    scalep,
    load_sem,
    small_sem,
    setup_send,
    setup_recv,
    ans_ssem,
    ans_rsem,
    g_ssem,
    g_rsem,
    f_ssem,
    f_rsem,
    halo_ssem,
    halo_rsem,
):
    r = lax.axis_index("region")
    c = lax.axis_index("blk")
    me = r * COLUMNS + c

    def peer(i):
        p = jnp.bitwise_xor(me, i)
        return p, (lax.shift_right_logical(p, 5), jnp.bitwise_and(p, COLUMNS - 1))

    def all_peers(step):
        for base in FAR_GROUPS:
            if base:
                lax.fori_loop(0, 8, lambda w, z: (step(base + jnp.bitwise_xor(w, 4)), z)[1], 0)
            else:
                for w in (0, 1, 2, 3, 5, 6, 7):
                    step(w ^ 4)

    def column_peers(step):
        far = 20
        lax.fori_loop(0, far, lambda w, z: (step(jnp.bitwise_xor(w, far)), z)[1], 0)
        lax.fori_loop(far + 1, COLUMNS, lambda w, z: (step(jnp.bitwise_xor(w, far)), z)[1], 0)

    def push(src, dst, ssem, rsem, where):
        pltpu.make_async_remote_copy(
            src_ref=src,
            dst_ref=dst,
            send_sem=ssem,
            recv_sem=rsem,
            device_id=where,
            device_id_type=MESH,
        ).start()

    def drain(ref, sem):
        pltpu.make_async_copy(ref, ref, sem).wait()

    barrier = pltpu.get_barrier_semaphore()

    def greet(i):
        pl.semaphore_signal(barrier, inc=1, device_id=peer(i)[1], device_id_type=MESH)

    all_peers(greet)

    cond_load = pltpu.make_async_copy(cond_hbm, cb, load_sem.at[0])
    view_load = pltpu.make_async_copy(view_hbm, vb, load_sem.at[1])
    pairs = [
        (dest_hbm, dest_ref),
        (node_hbm, node_ref),
        (emis_hbm, emis_ref),
        (temp_hbm, temps),
        (vrow_hbm, vrow_ref),
        (vcol_hbm, vcol_ref),
        (frac_hbm, frac_ref),
        (crow_hbm, crow_ref),
        (ccol_hbm, ccol_ref),
        (scale_hbm, scale_ref),
        (absorb_hbm, absorb_ref),
        (diag_hbm, diag_ref),
        (source_hbm, source_ref),
    ]
    small = [
        pltpu.make_async_copy(src, dst, small_sem.at[n]) for n, (src, dst) in enumerate(pairs)
    ]
    for load in small:
        load.start()
    cond_load.start()
    view_load.start()

    for load in small:
        load.wait()

    emf[...] = emis_ref[...].astype(F32)
    upper_tri = pick(iota((VIEW, VIEW), 0) < iota((VIEW, VIEW), 1))
    peer_row = iota((PEERS, VIEW), 0)
    slot_row = iota((2 * CAP, VIEW), 0)
    slot_rank = jnp.bitwise_and(slot_row, CAP - 1)
    slot_low = slot_row < CAP

    def route(u, carry):
        count, first, second = carry
        dest = dest_ref[u]
        node = node_ref[pl.ds(u, 1), :]
        hit = jnp.where(peer_row == dest, 1.0, 0.0)
        hit16 = hit.astype(BF16)
        before = mm(hit16, upper_tri)
        rank = jnp.sum(hit * (before + count), axis=0, keepdims=True).astype(I32)
        code_mine[pl.ds(u, 1), :] = dest * CAP + rank
        ohd[r * RB + u] = hit16
        high = (lax.shift_right_logical(node, 7) + 1).astype(F32)
        low = jnp.bitwise_and(node, TILE - 1).astype(F32)
        match = slot_rank == rank
        one = jnp.where(match, jnp.where(slot_low, high, emf[pl.ds(u, 1), :]), 0.0)
        two = jnp.where(match & slot_low, low, 0.0)
        first = first + mm_nt(hit16, one.astype(BF16))
        second = second + mm_nt(hit16, two.astype(BF16))
        count = count + hit[:, VIEW - 1 :] + before[:, VIEW - 1 :]
        return count, first, second

    zero_rows = jnp.zeros((PEERS, 2 * CAP), F32)
    _, first, second = lax.fori_loop(
        0, RB, route, (jnp.zeros((PEERS, 1), F32), zero_rows, zero_rows), unroll=2
    )
    lane_low = iota((PEERS, 2 * CAP), 1) < CAP
    req_send[:, 0, :] = first * jnp.where(lane_low, 128.0, 1.0) + second
    req_send[:, 1, :] = zero_rows

    pads[...] = jnp.full((8, CPAD), -1, I32)
    pads[0:1, 0:VIEWS] = vrow_ref[...]
    pads[1:2, 0:VIEWS] = vcol_ref[...]
    pads[2:3, 0:CONDS] = crow_ref[...]
    pads[3:4, 0:CONDS] = ccol_ref[...]
    vrow = pads[0:1, 0:KPAD]
    vcol = pads[1:2, 0:KPAD]
    crow = pads[2:3, :]
    ccol = pads[3:4, :]
    owner = lax.shift_right_arithmetic(vrow, 4)
    offset = jnp.bitwise_and(vrow, RB - 1)
    owner_hit = pick(iota((COLUMNS, KPAD), 0) == owner)
    offset_hit = jnp.where(iota((128, KPAD), 0) == offset, 1.0, 0.0)
    present = jnp.where(mm_nt(owner_hit, offset_hit.astype(BF16)) > 0.5, 1.0, 0.0)
    tri128 = pick(iota((128, 128), 0) < iota((128, 128), 1))
    place = mm(present.astype(BF16), tri128)
    place_of = mm_tn(place.astype(BF16), owner_hit)
    slot = owner * SLOTS + jnp.sum(offset_hit * place_of, axis=0, keepdims=True).astype(I32)
    ohslot[...] = pick(iota((COLUMNS * SLOTS, KPAD), 0) == slot)
    slot_lane = iota((COLUMNS, 128), 1)
    lane_slot = jnp.bitwise_and(slot_lane, SLOTS - 1).astype(F32)
    table = jnp.zeros((COLUMNS, 128), F32)
    for f in range(RB):
        held = jnp.where(present[:, f : f + 1] > 0.5, place[:, f : f + 1], -1.0)
        table = table + jnp.where(lane_slot == held, f + 1.0, 0.0)
    own_lanes = lax.shift_right_logical(slot_lane, 3) == jnp.bitwise_and(c, 15)
    req_send[pl.ds(r * COLUMNS, COLUMNS), 1, :] = jnp.where(own_lanes, table, 0.0)

    for b in range(BANDS):
        frac_mine[b] = frac_ref[:, b, :]
    ohcol = pick(iota((GROUP, KPAD), 0) == vcol)
    scalep[...] = jnp.zeros((8, KPAD), F32)
    scalep[0:BANDS, 0:VIEWS] = scale_ref[...]
    terms[...] = jnp.zeros((CPAD, TILE), F32)
    oh_ctile = pick(iota((TILES, CPAD), 0) == crow)
    ccol_at = jnp.where(ccol == 0, TILES, jnp.where(ccol == TILES + 1, TILES + 1, ccol - 1))
    oh_ccol = pick(iota((TILES + 16, CPAD), 0) == jnp.where(ccol < 0, -1, ccol_at))

    pl.semaphore_wait(barrier, PEERS - 1)

    mine = pl.ds(pl.multiple_of(r * RB, RB), RB)
    def send_request(i):
        p, where = peer(i)
        push(req_send.at[p], req_recv.at[me], setup_send.at[0], setup_recv.at[0], where)

    all_peers(send_request)
    for i in range(1, REGIONS):
        where = (jnp.bitwise_xor(r, i), c)
        push(code_mine, code_all.at[mine], setup_send.at[1], setup_recv.at[1], where)
    req_recv[pl.ds(me, 1)] = req_send[pl.ds(me, 1)]
    code_all[mine, :] = code_mine[...]
    frac_all[:, mine, :] = frac_mine[...]

    after = lax.rem(me + 1, PEERS)
    ahead = lax.rem(me + PEERS - 1, PEERS)
    after_id = (lax.shift_right_logical(after, 5), jnp.bitwise_and(after, COLUMNS - 1))
    ahead_id = (lax.shift_right_logical(ahead, 5), jnp.bitwise_and(ahead, COLUMNS - 1))

    def send_halo(it):
        halo_send[it, 0] = temps[TILES - 1 :, :]
        halo_send[it, 1] = temps[0:1, :]
        push(
            halo_send.at[it, 0], halo_recv.at[it, 0], halo_ssem.at[it, 0], halo_rsem.at[it, 0], after_id
        )
        push(
            halo_send.at[it, 1], halo_recv.at[it, 1], halo_ssem.at[it, 1], halo_rsem.at[it, 1], ahead_id
        )

    def wait_halo(it):
        for s in range(2):
            drain(halo_recv.at[it, s], halo_rsem.at[it, s])
            drain(halo_send.at[it, s], halo_ssem.at[it, s])

    send_halo(0)

    view_load.wait()

    def turn(k, carry):
        vb[k] = vb[k].T
        return carry

    lax.fori_loop(0, VIEWS, turn, 0, unroll=4)
    drain(req_recv.at[0 : PEERS - 1], setup_recv.at[0])
    drain(req_recv.at[0 : PEERS - 1], setup_send.at[0])
    asked = req_recv[:, 0, :]
    code4 = rows_to_slots(asked, False).astype(I32)
    em4[...] = rows_to_slots(asked, True)
    hi4[...] = lax.shift_right_logical(code4, 7) - 1
    lo4[...] = jnp.bitwise_and(code4, TILE - 1)
    tile_row = iota((TILES, VIEW), 0)
    node_row = iota((TILE, VIEW), 0)

    def build_node(j, carry):
        ohlo[j] = pick(node_row == lo4[pl.ds(j, 1), :])
        return carry

    lax.fori_loop(0, COLUMNS, build_node, 0, unroll=4)

    def answer(it):
        up, down = halves(temps[...])
        both = jnp.concatenate([up, down], axis=0)

        def look(j, carry):
            found = mm(both, ohlo[j])
            found = found[0:TILES] + found[TILES:]
            ans_send[j] = jnp.sum(
                jnp.where(tile_row == hi4[pl.ds(j, 1), :], found, 0.0), axis=0, keepdims=True
            )
            return carry

        lax.fori_loop(0, COLUMNS, look, 0, unroll=16)

        def send(i):
            where = peer(i)[1]
            push(ans_send.at[where[1]], ans_recv.at[it, me], ans_ssem.at[it], ans_rsem.at[it], where)

        all_peers(send)
        ans_recv[it, pl.ds(me, 1)] = ans_send[pl.ds(c, 1)]

    def conduct(it):
        wait_halo(it)
        before = jnp.where(me == 0, 0.0, halo_recv[it, 0])
        behind = jnp.where(me == PEERS - 1, 0.0, halo_recv[it, 1])
        edge_row = iota((16, TILE), 0)
        edges = jnp.where(edge_row == 0, before, jnp.where(edge_row == 1, behind, 0.0))
        up, down = halves(jnp.concatenate([temps[...], edges], axis=0))
        colt[...] = mm_tn(oh_ccol, jnp.concatenate([up, down], axis=1))
        eight = iota((8, TILE), 0)

        def group(g, carry):
            rows = colt[pl.ds(pl.multiple_of(g * 8, 8), 8), :]
            left = jnp.concatenate([rows[:, 0:TILE], rows[:, TILE:]], axis=0).astype(BF16)
            total = jnp.zeros((8, TILE), F32)
            for a in range(8):
                part = mm_nt(left, cb[g * 8 + a])
                total = jnp.where(eight == a, part[0:8] + part[8:16], total)
            terms[pl.ds(pl.multiple_of(g * 8, 8), 8), :] = total
            return carry

        lax.fori_loop(0, CONDS // 8, group, 0)
        up, down = halves(terms[...])
        return mm(oh_ctile, up) + mm(oh_ctile, down)

    answer(0)
    for i in range(1, REGIONS):
        where = (jnp.bitwise_xor(r, i), c)
        push(frac_mine, frac_all.at[:, mine, :], setup_send.at[2], setup_recv.at[2], where)
    others = pl.ds(0, (REGIONS - 1) * RB)
    drain(code_all.at[others], setup_recv.at[1])
    drain(code_all.at[others], setup_send.at[1])

    def build_dest(n, carry):
        q = lax.rem(n + (r + 1) * RB, GROUP)
        ohd[q] = pick(peer_row == lax.shift_right_logical(code_all[pl.ds(q, 1), :], 6))
        return carry

    lax.fori_loop(0, GROUP - RB, build_dest, 0, unroll=8)

    codes = req_recv[pl.ds(r * COLUMNS, COLUMNS), 1, :]
    row_codes = jnp.concatenate(
        [
            jnp.sum(codes[0:16], axis=0, keepdims=True),
            jnp.sum(codes[16:32], axis=0, keepdims=True),
        ],
        axis=1,
    ).astype(I32)
    ohrow = pick(iota((RB, COLUMNS * SLOTS), 0) + 1 == row_codes)
    for b in range(0, BANDS, 2):
        pair = [
            mm_tn(ohrow, absorb_ref[:, b + i, :]).reshape(COLUMNS, SLOTS, VIEW) for i in range(2)
        ]
        ab_send[:, b * SLOTS : (b + 2) * SLOTS, :] = jnp.concatenate(pair, axis=1).astype(BF16)

    def gather_emis(j, acc):
        spread = jnp.where(tile_row == hi4[pl.ds(j, 1), :], em4[pl.ds(j, 1), :], 0.0)
        return acc + mm_nt(spread.astype(BF16), ohlo[j])

    esum[...] = lax.fori_loop(0, COLUMNS, gather_emis, jnp.zeros((TILES, TILE), F32), unroll=4)

    def send_absorb(i):
        p = jnp.bitwise_xor(c, i)
        push(ab_send.at[p], ab_recv.at[c], setup_send.at[3], setup_recv.at[3], (r, p))

    column_peers(send_absorb)
    ab_recv[pl.ds(c, 1)] = ab_send[pl.ds(c, 1)]
    drain(frac_all.at[:, others, :], setup_recv.at[2])
    drain(frac_all.at[:, others, :], setup_send.at[2])
    rank_row = iota((CAP, VIEW), 0)

    for it in range(ITERS):
        if it > 0:
            answer(it)
        drain(ans_recv.at[it, 0 : PEERS - 1], ans_rsem.at[it])
        drain(ans_recv.at[it, 0 : PEERS - 1], ans_ssem.at[it])
        up, down = halves(ans_recv[it, :, 0, :].T)
        for i in range(REGIONS):
            span = slice(i * CAP, (i + 1) * CAP)
            ftl[i] = jnp.concatenate([up[span], down[span]], axis=0)

        def unpack(q, carry):
            found = mm(ftl[lax.shift_right_logical(q, 4)], ohd[q])
            found = found[0:CAP] + found[CAP:]
            rank = jnp.bitwise_and(code_all[pl.ds(q, 1), :], CAP - 1)
            value = jnp.sum(jnp.where(rank_row == rank, found, 0.0), axis=0, keepdims=True)
            squared = value * value
            patchq[pl.ds(q, 1), :] = squared * squared
            return carry

        lax.fori_loop(0, GROUP, unpack, 0, unroll=32)
        quartic = patchq[...]
        for b in range(BANDS):
            emit = (frac_all[b].astype(F32) * quartic).astype(BF16)
            ecol[b] = mm_tn(ohcol, emit)
        def view(k, carry):
            prod[:, k, :] = mm(ecol[:, k, :].astype(BF16), vb[k])
            return carry

        lax.fori_loop(0, VIEWS, view, 0, unroll=32)
        if it == 0:
            drain(ab_recv.at[0 : COLUMNS - 1], setup_recv.at[3])
            drain(ab_recv.at[0 : COLUMNS - 1], setup_send.at[3])
            rows = ab_recv[...].astype(F32)
            diagonal = iota((KPAD, KPAD), 0) == iota((KPAD, KPAD), 1)
            for b in range(BANDS):
                mine_b = rows[:, b * SLOTS : (b + 1) * SLOTS, :].reshape(COLUMNS * SLOTS, VIEW)
                column = jnp.sum(
                    jnp.where(diagonal, scalep[b : b + 1, :], 0.0), axis=1, keepdims=True
                )
                abk[b] = mm_tn(ohslot[...], mine_b.astype(BF16)) * column
        gained = prod[0] * abk[0, 0:VIEWS]
        for b in range(1, BANDS):
            gained = gained + prod[b] * abk[b, 0:VIEWS]
        up, down = halves(
            jnp.concatenate([gained, jnp.zeros((KPAD - VIEWS, VIEW), F32)], axis=0)
        )
        g_send[...] = (mm(ohslot[...], up) + mm(ohslot[...], down)).reshape(COLUMNS, SLOTS, VIEW)

        def send_rows(i):
            p = jnp.bitwise_xor(c, i)
            push(g_send.at[p], g_recv.at[it, c], g_ssem.at[it], g_rsem.at[it], (r, p))

        column_peers(send_rows)
        g_recv[it, pl.ds(c, 1)] = g_send[pl.ds(c, 1)]
        if it == 0:
            cond_load.wait()
        conducted = conduct(it)
        drain(g_recv.at[it, 0 : COLUMNS - 1], g_rsem.at[it])
        drain(g_recv.at[it, 0 : COLUMNS - 1], g_ssem.at[it])
        up, down = halves(g_recv[it].reshape(COLUMNS * SLOTS, VIEW))
        flux = mm(ohrow, up) + mm(ohrow, down) - emf[...] * patchq[mine, :]
        flux_out[...] = flux
        up, down = halves(flux)
        up, down = up.astype(F32), down.astype(F32)
        packed = jnp.zeros((PEERS, 2 * CAP), F32)
        for first_row in range(0, RB, 8):
            left, right = [], []
            for u in range(first_row, first_row + 8):
                rank = jnp.bitwise_and(code_mine[u : u + 1, :], CAP - 1)
                spread = jnp.where(
                    slot_rank == rank, jnp.where(slot_low, up[u : u + 1], down[u : u + 1]), 0.0
                )
                left.append(ohd[r * RB + u])
                right.append(spread.astype(BF16))
            packed = packed + mm_nt(jnp.concatenate(left, axis=1), jnp.concatenate(right, axis=1))
        f_send[:, 0, :] = packed

        def send_flux(i):
            p, where = peer(i)
            push(f_send.at[p], f_recv.at[it, me], f_ssem.at[it], f_rsem.at[it], where)

        all_peers(send_flux)
        f_recv[it, pl.ds(me, 1)] = f_send[pl.ds(me, 1)]
        drain(f_recv.at[it, 0 : PEERS - 1], f_rsem.at[it])
        drain(f_recv.at[it, 0 : PEERS - 1], f_ssem.at[it])
        came = f_recv[it, :, 0, :]
        fh4[...] = rows_to_slots(came, False)
        fl4[...] = rows_to_slots(came, True)

        heat = jnp.zeros((2 * TILES, TILE), F32)
        for j in range(0, COLUMNS, 8):
            left, right = [], []
            for n in range(j, j + 8):
                hit = tile_row == hi4[n : n + 1, :]
                up = jnp.where(hit, fh4[n : n + 1, :], 0.0).astype(BF16)
                down = jnp.where(hit, fl4[n : n + 1, :], 0.0).astype(BF16)
                left.append(jnp.concatenate([up, down], axis=0))
                right.append(ohlo[n])
            heat = heat + mm_nt(jnp.concatenate(left, axis=1), jnp.concatenate(right, axis=1))
        old = temps[...]
        residual = (
            diag_ref[...] * old - conducted - (heat[0:TILES] + heat[TILES:]) - source_ref[...]
        )
        magnitude = jnp.abs(old)
        new = old - residual / (
            diag_ref[...] + 4.0 * magnitude * magnitude * magnitude * esum[...]
        )
        if it + 1 < ITERS:
            temps[...] = new
            send_halo(it + 1)
        else:
            node_out[...] = new


def shards(
    node_temp,
    node_diag,
    node_source,
    cond_blocks,
    cond_rows,
    cond_cols,
    view_blocks,
    view_scales,
    view_rows,
    view_cols,
    band_frac,
    absorb,
    emis,
    patch_dest,
    patch_node,
):
    vmem = pl.BlockSpec(memory_space=pltpu.VMEM)
    hbm = pl.BlockSpec(memory_space=pltpu.HBM)
    dma = pltpu.SemaphoreType.DMA
    node_final, patch_flux = pl.pallas_call(
        kernel,
        out_shape=(
            jax.ShapeDtypeStruct((TILES, TILE), F32),
            jax.ShapeDtypeStruct((RB, VIEW), F32),
        ),
        in_specs=[hbm] * 15,
        out_specs=(vmem, vmem),
        scratch_shapes=[
            pltpu.VMEM((RB, 1, VIEW), I32),
            pltpu.VMEM((RB, VIEW), I32),
            pltpu.VMEM((RB, VIEW), BF16),
            pltpu.VMEM((TILES, TILE), F32),
            pltpu.VMEM((1, VIEWS), I32),
            pltpu.VMEM((1, VIEWS), I32),
            pltpu.VMEM((RB, BANDS, VIEW), BF16),
            pltpu.VMEM((1, CONDS), I32),
            pltpu.VMEM((1, CONDS), I32),
            pltpu.VMEM((BANDS, VIEWS), F32),
            pltpu.VMEM((RB, BANDS, VIEW), BF16),
            pltpu.VMEM((TILES, TILE), F32),
            pltpu.VMEM((TILES, TILE), F32),
            pltpu.VMEM((CONDS, TILE, TILE), BF16),
            pltpu.VMEM((VIEWS, VIEW, VIEW), BF16),
            pltpu.VMEM((GROUP, PEERS, VIEW), BF16),
            pltpu.VMEM((COLUMNS, TILE, VIEW), BF16),
            pltpu.VMEM((RB, VIEW), I32),
            pltpu.VMEM((GROUP, VIEW), I32),
            pltpu.VMEM((BANDS, RB, VIEW), BF16),
            pltpu.VMEM((BANDS, GROUP, VIEW), BF16),
            pltpu.VMEM((PEERS, 2, 2 * CAP), F32),
            pltpu.VMEM((PEERS, 2, 2 * CAP), F32),
            pltpu.VMEM((COLUMNS, 1, REGIONS * CAP), F32),
            pltpu.VMEM((ITERS, PEERS, 1, REGIONS * CAP), F32),
            pltpu.VMEM((COLUMNS, BANDS * SLOTS, VIEW), BF16),
            pltpu.VMEM((COLUMNS, BANDS * SLOTS, VIEW), BF16),
            pltpu.VMEM((COLUMNS, SLOTS, VIEW), F32),
            pltpu.VMEM((ITERS, COLUMNS, SLOTS, VIEW), F32),
            pltpu.VMEM((PEERS, 1, 2 * CAP), F32),
            pltpu.VMEM((ITERS, PEERS, 1, 2 * CAP), F32),
            pltpu.VMEM((ITERS, 2, 1, TILE), F32),
            pltpu.VMEM((ITERS, 2, 1, TILE), F32),
            pltpu.VMEM((RB, VIEW), F32),
            pltpu.VMEM((COLUMNS, REGIONS * CAP), I32),
            pltpu.VMEM((COLUMNS, REGIONS * CAP), I32),
            pltpu.VMEM((COLUMNS, REGIONS * CAP), F32),
            pltpu.VMEM((COLUMNS, REGIONS * CAP), F32),
            pltpu.VMEM((COLUMNS, REGIONS * CAP), F32),
            pltpu.VMEM((GROUP, VIEW), F32),
            pltpu.VMEM((REGIONS, 2 * CAP, PEERS), BF16),
            pltpu.VMEM((BANDS, KPAD, VIEW), F32),
            pltpu.VMEM((BANDS, VIEWS, VIEW), F32),
            pltpu.VMEM((BANDS, KPAD, VIEW), F32),
            pltpu.VMEM((COLUMNS * SLOTS, KPAD), BF16),
            pltpu.VMEM((CPAD, 2 * TILE), F32),
            pltpu.VMEM((CPAD, TILE), F32),
            pltpu.VMEM((TILES, TILE), F32),
            pltpu.VMEM((8, CPAD), I32),
            pltpu.VMEM((8, KPAD), F32),
            dma((2,)),
            dma((13,)),
            dma((4,)),
            dma((4,)),
            dma((ITERS,)),
            dma((ITERS,)),
            dma((ITERS,)),
            dma((ITERS,)),
            dma((ITERS,)),
            dma((ITERS,)),
            dma((ITERS, 2)),
            dma((ITERS, 2)),
        ],
        compiler_params=pltpu.CompilerParams(
            collective_id=0, has_side_effects=True, vmem_limit_bytes=64 * 1024 * 1024
        ),
    )(
        patch_dest.reshape(RB, 1, VIEW),
        patch_node,
        emis,
        node_temp.reshape(TILES, TILE),
        view_rows.reshape(1, VIEWS),
        view_cols.reshape(1, VIEWS),
        band_frac,
        cond_rows.reshape(1, CONDS),
        cond_cols.reshape(1, CONDS),
        view_scales.reshape(VIEWS, BANDS).T,
        absorb,
        node_diag.reshape(TILES, TILE),
        node_source.reshape(TILES, TILE),
        cond_blocks.reshape(CONDS, TILE, TILE),
        view_blocks.reshape(VIEWS, VIEW, VIEW),
    )
    return node_final.reshape(TILES * TILE), patch_flux


def solution(mesh):
    placed = (
        P(("region", "blk")),
        P(("region", "blk")),
        P(("region", "blk")),
        P("region", "blk", None, None, None),
        P("region", "blk", None),
        P("region", "blk", None),
        P("region", "blk", None, None, None),
        P("region", "blk", None, None),
        P("region", "blk", None),
        P("region", "blk", None),
        P(("region", "blk"), None, None),
        P(("region", "blk"), None, None),
        P(("region", "blk"), None),
        P(("region", "blk"), None, None),
        P(("region", "blk"), None),
    )
    return jax.shard_map(
        shards,
        mesh=mesh,
        in_specs=placed,
        out_specs=(P(("region", "blk")), P(("region", "blk"), None)),
        check_vma=False,
    )
```

```python
import functools

import jax
import jax.numpy as jnp
from jax import lax
from jax.experimental import pallas as pl
from jax.experimental.pallas import tpu as pltpu
from jax.sharding import PartitionSpec as P

ITERS = 2
REGIONS = 4
COLUMNS = 32
PEERS = REGIONS * COLUMNS
BANDS = 4
RB = 16
VIEW = 256
VIEWS = 96
KPAD = 128
GROUP = RB * REGIONS
SLOTS = 8
CAP = 64
TILES = 64
TILE = 128
CONDS = 192
CPAD = 256
TURNED = 56
MESH = pl.DeviceIdType.MESH
F32 = jnp.float32
BF16 = jnp.bfloat16
I32 = jnp.int32


FAR_GROUPS = [
    rx * 32 + z * 8
    for rx, z in sorted(
        ((rx, z) for rx in range(4) for z in range(4)),
        key=lambda g: -((0, 1, 2, 1)[g[0]] + (0, 1, 2, 1)[g[1]]),
    )
]


def mm(a, b):
    return jnp.dot(a, b, preferred_element_type=F32)


def mm_nt(a, b):
    return lax.dot_general(a, b, (((1,), (1,)), ((), ())), preferred_element_type=F32)


def mm_tn(a, b):
    return lax.dot_general(a, b, (((0,), (0,)), ((), ())), preferred_element_type=F32)


def iota(shape, dim):
    return lax.broadcasted_iota(I32, shape, dim)


def pick(mask):
    return jnp.where(mask, 1.0, 0.0).astype(BF16)


def halves(x):
    upper = x.astype(BF16)
    return upper, (x - upper.astype(F32)).astype(BF16)


def rows_to_slots(left, swap):
    low = iota((COLUMNS, 128), 1) < CAP
    part = [left[i * COLUMNS : (i + 1) * COLUMNS] for i in range(REGIONS)]
    pairs = []
    for i in range(0, REGIONS, 2):
        first, second = part[i], part[i + 1]
        if swap:
            first = pltpu.roll(first, CAP, 1)
        else:
            second = pltpu.roll(second, CAP, 1)
        pairs.append(jnp.where(low, first, second))
    return jnp.concatenate(pairs, axis=1)


def kernel(
    dest_hbm,
    node_hbm,
    emis_hbm,
    temp_hbm,
    vrow_hbm,
    vcol_hbm,
    frac_hbm,
    crow_hbm,
    ccol_hbm,
    scale_hbm,
    absorb_hbm,
    diag_hbm,
    source_hbm,
    cond_hbm,
    view_hbm,
    node_out,
    flux_out,
    dest_ref,
    node_ref,
    emis_ref,
    temps,
    vrow_ref,
    vcol_ref,
    frac_ref,
    crow_ref,
    ccol_ref,
    scale_ref,
    absorb_ref,
    diag_ref,
    source_ref,
    cb,
    vb,
    ohd,
    ohlo,
    code_mine,
    code_all,
    frac_mine,
    frac_all,
    req_send,
    req_recv,
    ans_send,
    ans_recv,
    ab_send,
    ab_recv,
    g_send,
    g_recv,
    f_send,
    f_recv,
    halo_send,
    halo_recv,
    emf,
    hi4,
    lo4,
    em4,
    fh4,
    fl4,
    patchq,
    ftl,
    ecol,
    prod,
    abk,
    ohslot,
    colt,
    terms,
    esum,
    pads,
    scalep,
    load_sem,
    small_sem,
    setup_send,
    setup_recv,
    ans_ssem,
    ans_rsem,
    g_ssem,
    g_rsem,
    f_ssem,
    f_rsem,
    halo_ssem,
    halo_rsem,
):
    r = lax.axis_index("region")
    c = lax.axis_index("blk")
    me = r * COLUMNS + c

    def peer(i):
        p = jnp.bitwise_xor(me, i)
        return p, (lax.shift_right_logical(p, 5), jnp.bitwise_and(p, COLUMNS - 1))

    def all_peers(step):
        for base in FAR_GROUPS:
            if base:
                lax.fori_loop(0, 8, lambda w, z: (step(base + jnp.bitwise_xor(w, 4)), z)[1], 0)
            else:
                for w in (0, 1, 2, 3, 5, 6, 7):
                    step(w ^ 4)

    def column_peers(step):
        far = 20
        lax.fori_loop(0, far, lambda w, z: (step(jnp.bitwise_xor(w, far)), z)[1], 0)
        lax.fori_loop(far + 1, COLUMNS, lambda w, z: (step(jnp.bitwise_xor(w, far)), z)[1], 0)

    def push(src, dst, ssem, rsem, where):
        pltpu.make_async_remote_copy(
            src_ref=src,
            dst_ref=dst,
            send_sem=ssem,
            recv_sem=rsem,
            device_id=where,
            device_id_type=MESH,
        ).start()

    def drain(ref, sem):
        pltpu.make_async_copy(ref, ref, sem).wait()

    barrier = pltpu.get_barrier_semaphore()

    def greet(i):
        pl.semaphore_signal(barrier, inc=1, device_id=peer(i)[1], device_id_type=MESH)

    all_peers(greet)

    cond_load = pltpu.make_async_copy(cond_hbm, cb, load_sem.at[0])
    view_load = pltpu.make_async_copy(view_hbm, vb, load_sem.at[1])
    pairs = [
        (dest_hbm, dest_ref),
        (node_hbm, node_ref),
        (emis_hbm, emis_ref),
        (temp_hbm, temps),
        (vrow_hbm, vrow_ref),
        (vcol_hbm, vcol_ref),
        (frac_hbm, frac_ref),
        (crow_hbm, crow_ref),
        (ccol_hbm, ccol_ref),
        (scale_hbm, scale_ref),
        (absorb_hbm, absorb_ref),
        (diag_hbm, diag_ref),
        (source_hbm, source_ref),
    ]
    small = [
        pltpu.make_async_copy(src, dst, small_sem.at[n]) for n, (src, dst) in enumerate(pairs)
    ]
    for load in small:
        load.start()
    cond_load.start()
    view_load.start()

    for load in small:
        load.wait()

    emf[...] = emis_ref[...].astype(F32)
    upper_tri = pick(iota((VIEW, VIEW), 0) < iota((VIEW, VIEW), 1))
    peer_row = iota((PEERS, VIEW), 0)
    slot_row = iota((2 * CAP, VIEW), 0)
    slot_rank = jnp.bitwise_and(slot_row, CAP - 1)
    slot_low = slot_row < CAP

    def route(u, carry):
        count, first, second = carry
        dest = dest_ref[u]
        node = node_ref[pl.ds(u, 1), :]
        hit = jnp.where(peer_row == dest, 1.0, 0.0)
        hit16 = hit.astype(BF16)
        before = mm(hit16, upper_tri)
        rank = jnp.sum(hit * (before + count), axis=0, keepdims=True).astype(I32)
        code_mine[pl.ds(u, 1), :] = dest * CAP + rank
        ohd[r * RB + u] = hit16
        high = (lax.shift_right_logical(node, 7) + 1).astype(F32)
        low = jnp.bitwise_and(node, TILE - 1).astype(F32)
        match = slot_rank == rank
        one = jnp.where(match, jnp.where(slot_low, high, emf[pl.ds(u, 1), :]), 0.0)
        two = jnp.where(match & slot_low, low, 0.0)
        first = first + mm_nt(hit16, one.astype(BF16))
        second = second + mm_nt(hit16, two.astype(BF16))
        count = count + hit[:, VIEW - 1 :] + before[:, VIEW - 1 :]
        return count, first, second

    zero_rows = jnp.zeros((PEERS, 2 * CAP), F32)
    _, first, second = lax.fori_loop(
        0, RB, route, (jnp.zeros((PEERS, 1), F32), zero_rows, zero_rows), unroll=2
    )
    lane_low = iota((PEERS, 2 * CAP), 1) < CAP
    req_send[:, 0, :] = first * jnp.where(lane_low, 128.0, 1.0) + second
    req_send[:, 1, :] = zero_rows

    pads[...] = jnp.full((8, CPAD), -1, I32)
    pads[0:1, 0:VIEWS] = vrow_ref[...]
    pads[1:2, 0:VIEWS] = vcol_ref[...]
    pads[2:3, 0:CONDS] = crow_ref[...]
    pads[3:4, 0:CONDS] = ccol_ref[...]
    vrow = pads[0:1, 0:KPAD]
    vcol = pads[1:2, 0:KPAD]
    crow = pads[2:3, :]
    ccol = pads[3:4, :]
    owner = lax.shift_right_arithmetic(vrow, 4)
    offset = jnp.bitwise_and(vrow, RB - 1)
    owner_hit = pick(iota((COLUMNS, KPAD), 0) == owner)
    offset_hit = jnp.where(iota((128, KPAD), 0) == offset, 1.0, 0.0)
    present = jnp.where(mm_nt(owner_hit, offset_hit.astype(BF16)) > 0.5, 1.0, 0.0)
    tri128 = pick(iota((128, 128), 0) < iota((128, 128), 1))
    place = mm(present.astype(BF16), tri128)
    place_of = mm_tn(place.astype(BF16), owner_hit)
    slot = owner * SLOTS + jnp.sum(offset_hit * place_of, axis=0, keepdims=True).astype(I32)
    ohslot[...] = pick(iota((COLUMNS * SLOTS, KPAD), 0) == slot)
    slot_lane = iota((COLUMNS, 128), 1)
    lane_slot = jnp.bitwise_and(slot_lane, SLOTS - 1).astype(F32)
    table = jnp.zeros((COLUMNS, 128), F32)
    for f in range(RB):
        held = jnp.where(present[:, f : f + 1] > 0.5, place[:, f : f + 1], -1.0)
        table = table + jnp.where(lane_slot == held, f + 1.0, 0.0)
    own_lanes = lax.shift_right_logical(slot_lane, 3) == jnp.bitwise_and(c, 15)
    req_send[pl.ds(r * COLUMNS, COLUMNS), 1, :] = jnp.where(own_lanes, table, 0.0)

    for b in range(BANDS):
        frac_mine[b] = frac_ref[:, b, :]
    ohcol = jnp.where(iota((KPAD, KPAD), 0) == vcol, 1.0, 0.0).T[:, 0:GROUP].astype(BF16)
    scalep[...] = jnp.zeros((8, KPAD), F32)
    scalep[0:BANDS, 0:VIEWS] = scale_ref[...]
    terms[...] = jnp.zeros((CPAD, TILE), F32)
    oh_ctile = pick(iota((TILES, CPAD), 0) == crow)
    ccol_at = jnp.where(ccol == 0, TILES, jnp.where(ccol == TILES + 1, TILES + 1, ccol - 1))
    oh_ccol = pick(iota((TILES + 16, CPAD), 0) == jnp.where(ccol < 0, -1, ccol_at))

    pl.semaphore_wait(barrier, PEERS - 1)

    mine = pl.ds(pl.multiple_of(r * RB, RB), RB)
    def send_request(i):
        p, where = peer(i)
        push(req_send.at[p], req_recv.at[me], setup_send.at[0], setup_recv.at[0], where)

    all_peers(send_request)
    for i in range(1, REGIONS):
        where = (jnp.bitwise_xor(r, i), c)
        push(code_mine, code_all.at[mine], setup_send.at[1], setup_recv.at[1], where)
    req_recv[pl.ds(me, 1)] = req_send[pl.ds(me, 1)]
    code_all[mine, :] = code_mine[...]
    frac_all[:, mine, :] = frac_mine[...]

    after = lax.rem(me + 1, PEERS)
    ahead = lax.rem(me + PEERS - 1, PEERS)
    after_id = (lax.shift_right_logical(after, 5), jnp.bitwise_and(after, COLUMNS - 1))
    ahead_id = (lax.shift_right_logical(ahead, 5), jnp.bitwise_and(ahead, COLUMNS - 1))

    def send_halo(it):
        halo_send[it, 0] = temps[TILES - 1 :, :]
        halo_send[it, 1] = temps[0:1, :]
        push(
            halo_send.at[it, 0], halo_recv.at[it, 0], halo_ssem.at[it, 0], halo_rsem.at[it, 0], after_id
        )
        push(
            halo_send.at[it, 1], halo_recv.at[it, 1], halo_ssem.at[it, 1], halo_rsem.at[it, 1], ahead_id
        )

    def wait_halo(it):
        for s in range(2):
            drain(halo_recv.at[it, s], halo_rsem.at[it, s])
            drain(halo_send.at[it, s], halo_ssem.at[it, s])

    send_halo(0)

    view_load.wait()

    def turn(k, carry):
        vb[k] = vb[k].T
        return carry

    lax.fori_loop(0, TURNED, turn, 0, unroll=4)
    drain(req_recv.at[0 : PEERS - 1], setup_recv.at[0])
    drain(req_recv.at[0 : PEERS - 1], setup_send.at[0])
    asked = req_recv[:, 0, :]
    code4 = rows_to_slots(asked, False).astype(I32)
    em4[...] = rows_to_slots(asked, True)
    hi4[...] = lax.shift_right_logical(code4, 7) - 1
    lo4[...] = jnp.bitwise_and(code4, TILE - 1)
    tile_row = iota((TILES, VIEW), 0)
    node_row = iota((TILE, VIEW), 0)

    def answer(it):
        up, down = halves(temps[...])
        both = jnp.concatenate([up, down], axis=0)

        def look(j, carry):
            if it == 0:
                hot = pick(node_row == lo4[pl.ds(j, 1), :])
                ohlo[j] = hot
            else:
                hot = ohlo[j]
            found = mm(both, hot)
            found = found[0:TILES] + found[TILES:]
            ans_send[j] = jnp.sum(
                jnp.where(tile_row == hi4[pl.ds(j, 1), :], found, 0.0), axis=0, keepdims=True
            )
            return carry

        lax.fori_loop(0, COLUMNS, look, 0, unroll=16)

        def send(i):
            where = peer(i)[1]
            push(ans_send.at[where[1]], ans_recv.at[it, me], ans_ssem.at[it], ans_rsem.at[it], where)

        all_peers(send)
        ans_recv[it, pl.ds(me, 1)] = ans_send[pl.ds(c, 1)]

    def conduct(it):
        wait_halo(it)
        before = jnp.where(me == 0, 0.0, halo_recv[it, 0])
        behind = jnp.where(me == PEERS - 1, 0.0, halo_recv[it, 1])
        edge_row = iota((16, TILE), 0)
        edges = jnp.where(edge_row == 0, before, jnp.where(edge_row == 1, behind, 0.0))
        up, down = halves(jnp.concatenate([temps[...], edges], axis=0))
        colt[...] = mm_tn(oh_ccol, jnp.concatenate([up, down], axis=1))
        eight = iota((8, TILE), 0)

        def group(g, carry):
            rows = colt[pl.ds(pl.multiple_of(g * 8, 8), 8), :]
            left = jnp.concatenate([rows[:, 0:TILE], rows[:, TILE:]], axis=0).astype(BF16)
            total = jnp.zeros((8, TILE), F32)
            for a in range(8):
                part = mm_nt(left, cb[g * 8 + a])
                total = jnp.where(eight == a, part[0:8] + part[8:16], total)
            terms[pl.ds(pl.multiple_of(g * 8, 8), 8), :] = total
            return carry

        lax.fori_loop(0, CONDS // 8, group, 0)
        up, down = halves(terms[...])
        return mm(oh_ctile, up) + mm(oh_ctile, down)

    answer(0)
    for i in range(1, REGIONS):
        where = (jnp.bitwise_xor(r, i), c)
        push(frac_mine, frac_all.at[:, mine, :], setup_send.at[2], setup_recv.at[2], where)
    others = pl.ds(0, (REGIONS - 1) * RB)
    drain(code_all.at[others], setup_recv.at[1])
    drain(code_all.at[others], setup_send.at[1])

    def build_dest(n, carry):
        q = lax.rem(n + (r + 1) * RB, GROUP)
        ohd[q] = pick(peer_row == lax.shift_right_logical(code_all[pl.ds(q, 1), :], 6))
        return carry

    lax.fori_loop(0, GROUP - RB, build_dest, 0, unroll=8)

    codes = req_recv[pl.ds(r * COLUMNS, COLUMNS), 1, :]
    row_codes = jnp.concatenate(
        [
            jnp.sum(codes[0:16], axis=0, keepdims=True),
            jnp.sum(codes[16:32], axis=0, keepdims=True),
        ],
        axis=1,
    ).astype(I32)
    ohrow = pick(iota((RB, COLUMNS * SLOTS), 0) + 1 == row_codes)
    for b in range(0, BANDS, 2):
        pair = [
            mm_tn(ohrow, absorb_ref[:, b + i, :]).reshape(COLUMNS, SLOTS, VIEW) for i in range(2)
        ]
        ab_send[:, b * SLOTS : (b + 2) * SLOTS, :] = jnp.concatenate(pair, axis=1).astype(BF16)

    def send_absorb(i):
        p = jnp.bitwise_xor(c, i)
        push(ab_send.at[p], ab_recv.at[c], setup_send.at[3], setup_recv.at[3], (r, p))

    column_peers(send_absorb)
    ab_recv[pl.ds(c, 1)] = ab_send[pl.ds(c, 1)]
    lax.fori_loop(TURNED, VIEWS, turn, 0, unroll=4)
    drain(frac_all.at[:, others, :], setup_recv.at[2])
    drain(frac_all.at[:, others, :], setup_send.at[2])
    rank_row = iota((CAP, VIEW), 0)

    for it in range(ITERS):
        if it > 0:
            answer(it)
        drain(ans_recv.at[it, 0 : PEERS - 1], ans_rsem.at[it])
        drain(ans_recv.at[it, 0 : PEERS - 1], ans_ssem.at[it])
        up, down = halves(ans_recv[it, :, 0, :].T)
        for i in range(REGIONS):
            span = slice(i * CAP, (i + 1) * CAP)
            ftl[i] = jnp.concatenate([up[span], down[span]], axis=0)

        def unpack(q, carry):
            found = mm(ftl[lax.shift_right_logical(q, 4)], ohd[q])
            found = found[0:CAP] + found[CAP:]
            rank = jnp.bitwise_and(code_all[pl.ds(q, 1), :], CAP - 1)
            value = jnp.sum(jnp.where(rank_row == rank, found, 0.0), axis=0, keepdims=True)
            squared = value * value
            patchq[pl.ds(q, 1), :] = squared * squared
            return carry

        lax.fori_loop(0, GROUP, unpack, 0, unroll=32)
        quartic = patchq[...]
        for b in range(BANDS):
            emit = (frac_all[b].astype(F32) * quartic).astype(BF16)
            ecol[b] = mm(ohcol, emit)
        def view(k, carry):
            prod[:, k, :] = mm(ecol[:, k, :].astype(BF16), vb[k])
            return carry

        lax.fori_loop(0, VIEWS, view, 0, unroll=32)
        if it == 0:
            drain(ab_recv.at[0 : COLUMNS - 1], setup_recv.at[3])
            drain(ab_recv.at[0 : COLUMNS - 1], setup_send.at[3])
            rows = ab_recv[...].astype(F32)
            diagonal = iota((KPAD, KPAD), 0) == iota((KPAD, KPAD), 1)
            for b in range(BANDS):
                mine_b = rows[:, b * SLOTS : (b + 1) * SLOTS, :].reshape(COLUMNS * SLOTS, VIEW)
                column = jnp.sum(
                    jnp.where(diagonal, scalep[b : b + 1, :], 0.0), axis=1, keepdims=True
                )
                abk[b] = mm_tn(ohslot[...], mine_b.astype(BF16)) * column
        gained = prod[0] * abk[0, 0:VIEWS]
        for b in range(1, BANDS):
            gained = gained + prod[b] * abk[b, 0:VIEWS]
        up, down = halves(
            jnp.concatenate([gained, jnp.zeros((KPAD - VIEWS, VIEW), F32)], axis=0)
        )
        g_send[...] = (mm(ohslot[...], up) + mm(ohslot[...], down)).reshape(COLUMNS, SLOTS, VIEW)

        def send_rows(i):
            p = jnp.bitwise_xor(c, i)
            push(g_send.at[p], g_recv.at[it, c], g_ssem.at[it], g_rsem.at[it], (r, p))

        column_peers(send_rows)
        g_recv[it, pl.ds(c, 1)] = g_send[pl.ds(c, 1)]
        if it == 0:
            cond_load.wait()
        conducted = conduct(it)
        drain(g_recv.at[it, 0 : COLUMNS - 1], g_rsem.at[it])
        drain(g_recv.at[it, 0 : COLUMNS - 1], g_ssem.at[it])
        up, down = halves(g_recv[it].reshape(COLUMNS * SLOTS, VIEW))
        flux = mm(ohrow, up) + mm(ohrow, down) - emf[...] * patchq[mine, :]
        flux_out[...] = flux
        up, down = halves(flux)
        up, down = up.astype(F32), down.astype(F32)
        packed = jnp.zeros((PEERS, 2 * CAP), F32)
        for first_row in range(0, RB, 8):
            left, right = [], []
            for u in range(first_row, first_row + 8):
                rank = jnp.bitwise_and(code_mine[u : u + 1, :], CAP - 1)
                spread = jnp.where(
                    slot_rank == rank, jnp.where(slot_low, up[u : u + 1], down[u : u + 1]), 0.0
                )
                left.append(ohd[r * RB + u])
                right.append(spread.astype(BF16))
            packed = packed + mm_nt(jnp.concatenate(left, axis=1), jnp.concatenate(right, axis=1))
        f_send[:, 0, :] = packed

        def send_flux(i):
            p, where = peer(i)
            push(f_send.at[p], f_recv.at[it, me], f_ssem.at[it], f_rsem.at[it], where)

        all_peers(send_flux)
        f_recv[it, pl.ds(me, 1)] = f_send[pl.ds(me, 1)]
        if it == 0:
            weight = jnp.zeros((TILES, TILE), F32)
            for j in range(0, COLUMNS, 8):
                left, right = [], []
                for n in range(j, j + 8):
                    hit = tile_row == hi4[n : n + 1, :]
                    left.append(jnp.where(hit, em4[n : n + 1, :], 0.0).astype(BF16))
                    right.append(ohlo[n])
                weight = weight + mm_nt(
                    jnp.concatenate(left, axis=1), jnp.concatenate(right, axis=1)
                )
            esum[...] = weight
        drain(f_recv.at[it, 0 : PEERS - 1], f_rsem.at[it])
        drain(f_recv.at[it, 0 : PEERS - 1], f_ssem.at[it])
        came = f_recv[it, :, 0, :]
        fh4[...] = rows_to_slots(came, False)
        fl4[...] = rows_to_slots(came, True)

        heat = jnp.zeros((2 * TILES, TILE), F32)
        for j in range(0, COLUMNS, 8):
            left, right = [], []
            for n in range(j, j + 8):
                hit = tile_row == hi4[n : n + 1, :]
                up = jnp.where(hit, fh4[n : n + 1, :], 0.0).astype(BF16)
                down = jnp.where(hit, fl4[n : n + 1, :], 0.0).astype(BF16)
                left.append(jnp.concatenate([up, down], axis=0))
                right.append(ohlo[n])
            heat = heat + mm_nt(jnp.concatenate(left, axis=1), jnp.concatenate(right, axis=1))
        old = temps[...]
        residual = (
            diag_ref[...] * old - conducted - (heat[0:TILES] + heat[TILES:]) - source_ref[...]
        )
        magnitude = jnp.abs(old)
        new = old - residual / (
            diag_ref[...] + 4.0 * magnitude * magnitude * magnitude * esum[...]
        )
        if it + 1 < ITERS:
            temps[...] = new
            send_halo(it + 1)
        else:
            node_out[...] = new


def shards(
    node_temp,
    node_diag,
    node_source,
    cond_blocks,
    cond_rows,
    cond_cols,
    view_blocks,
    view_scales,
    view_rows,
    view_cols,
    band_frac,
    absorb,
    emis,
    patch_dest,
    patch_node,
):
    vmem = pl.BlockSpec(memory_space=pltpu.VMEM)
    hbm = pl.BlockSpec(memory_space=pltpu.HBM)
    dma = pltpu.SemaphoreType.DMA
    node_final, patch_flux = pl.pallas_call(
        kernel,
        out_shape=(
            jax.ShapeDtypeStruct((TILES, TILE), F32),
            jax.ShapeDtypeStruct((RB, VIEW), F32),
        ),
        in_specs=[hbm] * 15,
        out_specs=(vmem, vmem),
        scratch_shapes=[
            pltpu.VMEM((RB, 1, VIEW), I32),
            pltpu.VMEM((RB, VIEW), I32),
            pltpu.VMEM((RB, VIEW), BF16),
            pltpu.VMEM((TILES, TILE), F32),
            pltpu.VMEM((1, VIEWS), I32),
            pltpu.VMEM((1, VIEWS), I32),
            pltpu.VMEM((RB, BANDS, VIEW), BF16),
            pltpu.VMEM((1, CONDS), I32),
            pltpu.VMEM((1, CONDS), I32),
            pltpu.VMEM((BANDS, VIEWS), F32),
            pltpu.VMEM((RB, BANDS, VIEW), BF16),
            pltpu.VMEM((TILES, TILE), F32),
            pltpu.VMEM((TILES, TILE), F32),
            pltpu.VMEM((CONDS, TILE, TILE), BF16),
            pltpu.VMEM((VIEWS, VIEW, VIEW), BF16),
            pltpu.VMEM((GROUP, PEERS, VIEW), BF16),
            pltpu.VMEM((COLUMNS, TILE, VIEW), BF16),
            pltpu.VMEM((RB, VIEW), I32),
            pltpu.VMEM((GROUP, VIEW), I32),
            pltpu.VMEM((BANDS, RB, VIEW), BF16),
            pltpu.VMEM((BANDS, GROUP, VIEW), BF16),
            pltpu.VMEM((PEERS, 2, 2 * CAP), F32),
            pltpu.VMEM((PEERS, 2, 2 * CAP), F32),
            pltpu.VMEM((COLUMNS, 1, REGIONS * CAP), F32),
            pltpu.VMEM((ITERS, PEERS, 1, REGIONS * CAP), F32),
            pltpu.VMEM((COLUMNS, BANDS * SLOTS, VIEW), BF16),
            pltpu.VMEM((COLUMNS, BANDS * SLOTS, VIEW), BF16),
            pltpu.VMEM((COLUMNS, SLOTS, VIEW), F32),
            pltpu.VMEM((ITERS, COLUMNS, SLOTS, VIEW), F32),
            pltpu.VMEM((PEERS, 1, 2 * CAP), F32),
            pltpu.VMEM((ITERS, PEERS, 1, 2 * CAP), F32),
            pltpu.VMEM((ITERS, 2, 1, TILE), F32),
            pltpu.VMEM((ITERS, 2, 1, TILE), F32),
            pltpu.VMEM((RB, VIEW), F32),
            pltpu.VMEM((COLUMNS, REGIONS * CAP), I32),
            pltpu.VMEM((COLUMNS, REGIONS * CAP), I32),
            pltpu.VMEM((COLUMNS, REGIONS * CAP), F32),
            pltpu.VMEM((COLUMNS, REGIONS * CAP), F32),
            pltpu.VMEM((COLUMNS, REGIONS * CAP), F32),
            pltpu.VMEM((GROUP, VIEW), F32),
            pltpu.VMEM((REGIONS, 2 * CAP, PEERS), BF16),
            pltpu.VMEM((BANDS, KPAD, VIEW), F32),
            pltpu.VMEM((BANDS, VIEWS, VIEW), F32),
            pltpu.VMEM((BANDS, KPAD, VIEW), F32),
            pltpu.VMEM((COLUMNS * SLOTS, KPAD), BF16),
            pltpu.VMEM((CPAD, 2 * TILE), F32),
            pltpu.VMEM((CPAD, TILE), F32),
            pltpu.VMEM((TILES, TILE), F32),
            pltpu.VMEM((8, CPAD), I32),
            pltpu.VMEM((8, KPAD), F32),
            dma((2,)),
            dma((13,)),
            dma((4,)),
            dma((4,)),
            dma((ITERS,)),
            dma((ITERS,)),
            dma((ITERS,)),
            dma((ITERS,)),
            dma((ITERS,)),
            dma((ITERS,)),
            dma((ITERS, 2)),
            dma((ITERS, 2)),
        ],
        compiler_params=pltpu.CompilerParams(
            collective_id=0, has_side_effects=True, vmem_limit_bytes=64 * 1024 * 1024
        ),
    )(
        patch_dest.reshape(RB, 1, VIEW),
        patch_node,
        emis,
        node_temp.reshape(TILES, TILE),
        view_rows.reshape(1, VIEWS),
        view_cols.reshape(1, VIEWS),
        band_frac,
        cond_rows.reshape(1, CONDS),
        cond_cols.reshape(1, CONDS),
        view_scales.reshape(VIEWS, BANDS).T,
        absorb,
        node_diag.reshape(TILES, TILE),
        node_source.reshape(TILES, TILE),
        cond_blocks.reshape(CONDS, TILE, TILE),
        view_blocks.reshape(VIEWS, VIEW, VIEW),
    )
    return node_final.reshape(TILES * TILE), patch_flux


def solution(mesh):
    placed = (
        P(("region", "blk")),
        P(("region", "blk")),
        P(("region", "blk")),
        P("region", "blk", None, None, None),
        P("region", "blk", None),
        P("region", "blk", None),
        P("region", "blk", None, None, None),
        P("region", "blk", None, None),
        P("region", "blk", None),
        P("region", "blk", None),
        P(("region", "blk"), None, None),
        P(("region", "blk"), None, None),
        P(("region", "blk"), None),
        P(("region", "blk"), None, None),
        P(("region", "blk"), None),
    )
    return jax.shard_map(
        shards,
        mesh=mesh,
        in_specs=placed,
        out_specs=(P(("region", "blk")), P(("region", "blk"), None)),
        check_vma=False,
    )
```

```python
import functools

import jax
import jax.numpy as jnp
from jax import lax
from jax.experimental import pallas as pl
from jax.experimental.pallas import tpu as pltpu
from jax.sharding import PartitionSpec as P

ITERS = 2
REGIONS = 4
COLUMNS = 32
PEERS = REGIONS * COLUMNS
BANDS = 4
RB = 16
VIEW = 256
VIEWS = 96
KPAD = 128
GROUP = RB * REGIONS
SLOTS = 8
CAP = 64
TILES = 64
TILE = 128
CONDS = 192
CPAD = 256
TURNED = 56
LATE = 72
MESH = pl.DeviceIdType.MESH
F32 = jnp.float32
BF16 = jnp.bfloat16
I32 = jnp.int32


FAR_GROUPS = [
    rx * 32 + z * 8
    for rx, z in sorted(
        ((rx, z) for rx in range(4) for z in range(4)),
        key=lambda g: -((0, 1, 2, 1)[g[0]] + (0, 1, 2, 1)[g[1]]),
    )
]


def mm(a, b):
    return jnp.dot(a, b, preferred_element_type=F32)


def mm_nt(a, b):
    return lax.dot_general(a, b, (((1,), (1,)), ((), ())), preferred_element_type=F32)


def mm_tn(a, b):
    return lax.dot_general(a, b, (((0,), (0,)), ((), ())), preferred_element_type=F32)


def iota(shape, dim):
    return lax.broadcasted_iota(I32, shape, dim)


def pick(mask):
    return jnp.where(mask, 1.0, 0.0).astype(BF16)


def halves(x):
    upper = x.astype(BF16)
    return upper, (x - upper.astype(F32)).astype(BF16)


def rows_to_slots(left, swap):
    low = iota((COLUMNS, 128), 1) < CAP
    part = [left[i * COLUMNS : (i + 1) * COLUMNS] for i in range(REGIONS)]
    pairs = []
    for i in range(0, REGIONS, 2):
        first, second = part[i], part[i + 1]
        if swap:
            first = pltpu.roll(first, CAP, 1)
        else:
            second = pltpu.roll(second, CAP, 1)
        pairs.append(jnp.where(low, first, second))
    return jnp.concatenate(pairs, axis=1)


def kernel(
    dest_hbm,
    node_hbm,
    emis_hbm,
    temp_hbm,
    vrow_hbm,
    vcol_hbm,
    frac_hbm,
    crow_hbm,
    ccol_hbm,
    scale_hbm,
    absorb_hbm,
    diag_hbm,
    source_hbm,
    cond_hbm,
    view_hbm,
    node_out,
    flux_out,
    dest_ref,
    node_ref,
    emis_ref,
    temps,
    vrow_ref,
    vcol_ref,
    frac_ref,
    crow_ref,
    ccol_ref,
    scale_ref,
    absorb_ref,
    diag_ref,
    source_ref,
    cb,
    vb,
    ohd,
    ohlo,
    code_mine,
    code_all,
    frac_mine,
    frac_all,
    req_send,
    req_recv,
    ans_send,
    ans_recv,
    ab_send,
    ab_recv,
    g_send,
    g_recv,
    f_send,
    f_recv,
    halo_send,
    halo_recv,
    emf,
    hi4,
    lo4,
    em4,
    fh4,
    fl4,
    patchq,
    ftl,
    ecol,
    prod,
    abk,
    ohslot,
    colt,
    terms,
    esum,
    pads,
    scalep,
    load_sem,
    small_sem,
    setup_send,
    setup_recv,
    ans_ssem,
    ans_rsem,
    g_ssem,
    g_rsem,
    f_ssem,
    f_rsem,
    halo_ssem,
    halo_rsem,
):
    r = lax.axis_index("region")
    c = lax.axis_index("blk")
    me = r * COLUMNS + c

    def peer(i):
        p = jnp.bitwise_xor(me, i)
        return p, (lax.shift_right_logical(p, 5), jnp.bitwise_and(p, COLUMNS - 1))

    def all_peers(step):
        for base in FAR_GROUPS:
            if base:
                lax.fori_loop(0, 8, lambda w, z: (step(base + jnp.bitwise_xor(w, 4)), z)[1], 0)
            else:
                for w in (0, 1, 2, 3, 5, 6, 7):
                    step(w ^ 4)

    def column_peers(step):
        far = 20
        lax.fori_loop(0, far, lambda w, z: (step(jnp.bitwise_xor(w, far)), z)[1], 0)
        lax.fori_loop(far + 1, COLUMNS, lambda w, z: (step(jnp.bitwise_xor(w, far)), z)[1], 0)

    def push(src, dst, ssem, rsem, where):
        pltpu.make_async_remote_copy(
            src_ref=src,
            dst_ref=dst,
            send_sem=ssem,
            recv_sem=rsem,
            device_id=where,
            device_id_type=MESH,
        ).start()

    def drain(ref, sem):
        pltpu.make_async_copy(ref, ref, sem).wait()

    barrier = pltpu.get_barrier_semaphore()

    def greet(i):
        pl.semaphore_signal(barrier, inc=1, device_id=peer(i)[1], device_id_type=MESH)

    all_peers(greet)

    cond_load = pltpu.make_async_copy(cond_hbm, cb, load_sem.at[0])
    view_load = pltpu.make_async_copy(view_hbm, vb, load_sem.at[1])
    pairs = [
        (dest_hbm, dest_ref),
        (node_hbm, node_ref),
        (emis_hbm, emis_ref),
        (temp_hbm, temps),
        (vrow_hbm, vrow_ref),
        (vcol_hbm, vcol_ref),
        (frac_hbm, frac_ref),
        (crow_hbm, crow_ref),
        (ccol_hbm, ccol_ref),
        (scale_hbm, scale_ref),
        (absorb_hbm, absorb_ref),
        (diag_hbm, diag_ref),
        (source_hbm, source_ref),
    ]
    small = [
        pltpu.make_async_copy(src, dst, small_sem.at[n]) for n, (src, dst) in enumerate(pairs)
    ]
    for load in small:
        load.start()
    cond_load.start()
    view_load.start()

    for load in small:
        load.wait()

    emf[...] = emis_ref[...].astype(F32)
    upper_tri = pick(iota((VIEW, VIEW), 0) < iota((VIEW, VIEW), 1))
    peer_row = iota((PEERS, VIEW), 0)
    slot_row = iota((2 * CAP, VIEW), 0)
    slot_rank = jnp.bitwise_and(slot_row, CAP - 1)
    slot_low = slot_row < CAP

    def route(u, carry):
        count, first, second = carry
        dest = dest_ref[u]
        node = node_ref[pl.ds(u, 1), :]
        hit = jnp.where(peer_row == dest, 1.0, 0.0)
        hit16 = hit.astype(BF16)
        before = mm(hit16, upper_tri)
        rank = jnp.sum(hit * (before + count), axis=0, keepdims=True).astype(I32)
        code_mine[pl.ds(u, 1), :] = dest * CAP + rank
        ohd[r * RB + u] = hit16
        high = (lax.shift_right_logical(node, 7) + 1).astype(F32)
        low = jnp.bitwise_and(node, TILE - 1).astype(F32)
        match = slot_rank == rank
        one = jnp.where(match, jnp.where(slot_low, high, emf[pl.ds(u, 1), :]), 0.0)
        two = jnp.where(match & slot_low, low, 0.0)
        first = first + mm_nt(hit16, one.astype(BF16))
        second = second + mm_nt(hit16, two.astype(BF16))
        count = count + hit[:, VIEW - 1 :] + before[:, VIEW - 1 :]
        return count, first, second

    zero_rows = jnp.zeros((PEERS, 2 * CAP), F32)
    _, first, second = lax.fori_loop(
        0, RB, route, (jnp.zeros((PEERS, 1), F32), zero_rows, zero_rows), unroll=2
    )
    lane_low = iota((PEERS, 2 * CAP), 1) < CAP
    req_send[:, 0, :] = first * jnp.where(lane_low, 128.0, 1.0) + second
    req_send[:, 1, :] = zero_rows

    pads[...] = jnp.full((8, CPAD), -1, I32)
    pads[0:1, 0:VIEWS] = vrow_ref[...]
    pads[1:2, 0:VIEWS] = vcol_ref[...]
    pads[2:3, 0:CONDS] = crow_ref[...]
    pads[3:4, 0:CONDS] = ccol_ref[...]
    vrow = pads[0:1, 0:KPAD]
    vcol = pads[1:2, 0:KPAD]
    crow = pads[2:3, :]
    ccol = pads[3:4, :]
    owner = lax.shift_right_arithmetic(vrow, 4)
    offset = jnp.bitwise_and(vrow, RB - 1)
    owner_hit = pick(iota((COLUMNS, KPAD), 0) == owner)
    offset_hit = jnp.where(iota((128, KPAD), 0) == offset, 1.0, 0.0)
    present = jnp.where(mm_nt(owner_hit, offset_hit.astype(BF16)) > 0.5, 1.0, 0.0)
    tri128 = pick(iota((128, 128), 0) < iota((128, 128), 1))
    place = mm(present.astype(BF16), tri128)
    place_of = mm_tn(place.astype(BF16), owner_hit)
    slot = owner * SLOTS + jnp.sum(offset_hit * place_of, axis=0, keepdims=True).astype(I32)
    ohslot[...] = pick(iota((COLUMNS * SLOTS, KPAD), 0) == slot)
    slot_lane = iota((COLUMNS, 128), 1)
    lane_slot = jnp.bitwise_and(slot_lane, SLOTS - 1).astype(F32)
    table = jnp.zeros((COLUMNS, 128), F32)
    for f in range(RB):
        held = jnp.where(present[:, f : f + 1] > 0.5, place[:, f : f + 1], -1.0)
        table = table + jnp.where(lane_slot == held, f + 1.0, 0.0)
    own_lanes = lax.shift_right_logical(slot_lane, 3) == jnp.bitwise_and(c, 15)
    req_send[pl.ds(r * COLUMNS, COLUMNS), 1, :] = jnp.where(own_lanes, table, 0.0)

    for b in range(BANDS):
        frac_mine[b] = frac_ref[:, b, :]
    ohcol = jnp.where(iota((KPAD, KPAD), 0) == vcol, 1.0, 0.0).T[:, 0:GROUP].astype(BF16)
    scalep[...] = jnp.zeros((8, KPAD), F32)
    scalep[0:BANDS, 0:VIEWS] = scale_ref[...]
    terms[...] = jnp.zeros((CPAD, TILE), F32)
    oh_ctile = pick(iota((TILES, CPAD), 0) == crow)
    ccol_at = jnp.where(ccol == 0, TILES, jnp.where(ccol == TILES + 1, TILES + 1, ccol - 1))
    oh_ccol = pick(iota((TILES + 16, CPAD), 0) == jnp.where(ccol < 0, -1, ccol_at))

    pl.semaphore_wait(barrier, PEERS - 1)

    mine = pl.ds(pl.multiple_of(r * RB, RB), RB)
    def send_request(i):
        p, where = peer(i)
        push(req_send.at[p], req_recv.at[me], setup_send.at[0], setup_recv.at[0], where)

    all_peers(send_request)
    for i in range(1, REGIONS):
        where = (jnp.bitwise_xor(r, i), c)
        push(code_mine, code_all.at[mine], setup_send.at[1], setup_recv.at[1], where)
    req_recv[pl.ds(me, 1)] = req_send[pl.ds(me, 1)]
    code_all[mine, :] = code_mine[...]
    frac_all[:, mine, :] = frac_mine[...]

    after = lax.rem(me + 1, PEERS)
    ahead = lax.rem(me + PEERS - 1, PEERS)
    after_id = (lax.shift_right_logical(after, 5), jnp.bitwise_and(after, COLUMNS - 1))
    ahead_id = (lax.shift_right_logical(ahead, 5), jnp.bitwise_and(ahead, COLUMNS - 1))

    def send_halo(it):
        halo_send[it, 0] = temps[TILES - 1 :, :]
        halo_send[it, 1] = temps[0:1, :]
        push(
            halo_send.at[it, 0], halo_recv.at[it, 0], halo_ssem.at[it, 0], halo_rsem.at[it, 0], after_id
        )
        push(
            halo_send.at[it, 1], halo_recv.at[it, 1], halo_ssem.at[it, 1], halo_rsem.at[it, 1], ahead_id
        )

    def wait_halo(it):
        for s in range(2):
            drain(halo_recv.at[it, s], halo_rsem.at[it, s])
            drain(halo_send.at[it, s], halo_ssem.at[it, s])

    send_halo(0)

    view_load.wait()

    def turn(k, carry):
        vb[k] = vb[k].T
        return carry

    lax.fori_loop(0, TURNED, turn, 0, unroll=4)
    drain(req_recv.at[0 : PEERS - 1], setup_recv.at[0])
    drain(req_recv.at[0 : PEERS - 1], setup_send.at[0])
    asked = req_recv[:, 0, :]
    code4 = rows_to_slots(asked, False).astype(I32)
    em4[...] = rows_to_slots(asked, True)
    hi4[...] = lax.shift_right_logical(code4, 7) - 1
    lo4[...] = jnp.bitwise_and(code4, TILE - 1)
    tile_row = iota((TILES, VIEW), 0)
    node_row = iota((TILE, VIEW), 0)

    def answer(it):
        up, down = halves(temps[...])
        both = jnp.concatenate([up, down], axis=0)

        def look(j, carry):
            if it == 0:
                hot = pick(node_row == lo4[pl.ds(j, 1), :])
                ohlo[j] = hot
            else:
                hot = ohlo[j]
            found = mm(both, hot)
            found = found[0:TILES] + found[TILES:]
            ans_send[j] = jnp.sum(
                jnp.where(tile_row == hi4[pl.ds(j, 1), :], found, 0.0), axis=0, keepdims=True
            )
            return carry

        lax.fori_loop(0, COLUMNS, look, 0, unroll=16)

        def send(i):
            where = peer(i)[1]
            push(ans_send.at[where[1]], ans_recv.at[it, me], ans_ssem.at[it], ans_rsem.at[it], where)

        all_peers(send)
        ans_recv[it, pl.ds(me, 1)] = ans_send[pl.ds(c, 1)]

    def conduct(it):
        wait_halo(it)
        before = jnp.where(me == 0, 0.0, halo_recv[it, 0])
        behind = jnp.where(me == PEERS - 1, 0.0, halo_recv[it, 1])
        edge_row = iota((16, TILE), 0)
        edges = jnp.where(edge_row == 0, before, jnp.where(edge_row == 1, behind, 0.0))
        up, down = halves(jnp.concatenate([temps[...], edges], axis=0))
        colt[...] = mm_tn(oh_ccol, jnp.concatenate([up, down], axis=1))
        eight = iota((8, TILE), 0)

        def group(g, carry):
            rows = colt[pl.ds(pl.multiple_of(g * 8, 8), 8), :]
            left = jnp.concatenate([rows[:, 0:TILE], rows[:, TILE:]], axis=0).astype(BF16)
            total = jnp.zeros((8, TILE), F32)
            for a in range(8):
                part = mm_nt(left, cb[g * 8 + a])
                total = jnp.where(eight == a, part[0:8] + part[8:16], total)
            terms[pl.ds(pl.multiple_of(g * 8, 8), 8), :] = total
            return carry

        lax.fori_loop(0, CONDS // 8, group, 0)
        up, down = halves(terms[...])
        return mm(oh_ctile, up) + mm(oh_ctile, down)

    answer(0)
    for i in range(1, REGIONS):
        where = (jnp.bitwise_xor(r, i), c)
        push(frac_mine, frac_all.at[:, mine, :], setup_send.at[2], setup_recv.at[2], where)
    codes = req_recv[pl.ds(r * COLUMNS, COLUMNS), 1, :]
    row_codes = jnp.concatenate(
        [
            jnp.sum(codes[0:16], axis=0, keepdims=True),
            jnp.sum(codes[16:32], axis=0, keepdims=True),
        ],
        axis=1,
    ).astype(I32)
    ohrow = pick(iota((RB, COLUMNS * SLOTS), 0) + 1 == row_codes)
    for b in range(0, BANDS, 2):
        pair = [
            mm_tn(ohrow, absorb_ref[:, b + i, :]).reshape(COLUMNS, SLOTS, VIEW) for i in range(2)
        ]
        ab_send[:, b * SLOTS : (b + 2) * SLOTS, :] = jnp.concatenate(pair, axis=1).astype(BF16)

    def send_absorb(i):
        p = jnp.bitwise_xor(c, i)
        push(ab_send.at[p], ab_recv.at[c], setup_send.at[3], setup_recv.at[3], (r, p))

    column_peers(send_absorb)
    ab_recv[pl.ds(c, 1)] = ab_send[pl.ds(c, 1)]
    others = pl.ds(0, (REGIONS - 1) * RB)
    drain(code_all.at[others], setup_recv.at[1])
    drain(code_all.at[others], setup_send.at[1])

    def build_dest(n, carry):
        q = lax.rem(n + (r + 1) * RB, GROUP)
        ohd[q] = pick(peer_row == lax.shift_right_logical(code_all[pl.ds(q, 1), :], 6))
        return carry

    lax.fori_loop(0, GROUP - RB, build_dest, 0, unroll=8)

    lax.fori_loop(TURNED, LATE, turn, 0, unroll=4)
    drain(frac_all.at[:, others, :], setup_recv.at[2])
    drain(frac_all.at[:, others, :], setup_send.at[2])
    rank_row = iota((CAP, VIEW), 0)

    for it in range(ITERS):
        if it > 0:
            answer(it)
        drain(ans_recv.at[it, 0 : PEERS - 1], ans_rsem.at[it])
        drain(ans_recv.at[it, 0 : PEERS - 1], ans_ssem.at[it])
        up, down = halves(ans_recv[it, :, 0, :].T)
        for i in range(REGIONS):
            span = slice(i * CAP, (i + 1) * CAP)
            ftl[i] = jnp.concatenate([up[span], down[span]], axis=0)

        def unpack(q, carry):
            found = mm(ftl[lax.shift_right_logical(q, 4)], ohd[q])
            found = found[0:CAP] + found[CAP:]
            rank = jnp.bitwise_and(code_all[pl.ds(q, 1), :], CAP - 1)
            value = jnp.sum(jnp.where(rank_row == rank, found, 0.0), axis=0, keepdims=True)
            squared = value * value
            patchq[pl.ds(q, 1), :] = squared * squared
            return carry

        lax.fori_loop(0, GROUP, unpack, 0, unroll=32)
        quartic = patchq[...]
        for b in range(BANDS):
            emit = (frac_all[b].astype(F32) * quartic).astype(BF16)
            ecol[b] = mm(ohcol, emit)
        def view(k, carry):
            prod[:, k, :] = mm(ecol[:, k, :].astype(BF16), vb[k])
            return carry

        def view_unturned(k, carry):
            prod[:, k, :] = mm_nt(ecol[:, k, :].astype(BF16), vb[k])
            return carry

        if it == 0:
            lax.fori_loop(0, LATE, view, 0, unroll=36)
            lax.fori_loop(LATE, VIEWS, view_unturned, 0, unroll=24)
        else:
            lax.fori_loop(0, VIEWS, view, 0, unroll=32)
        if it == 0:
            drain(ab_recv.at[0 : COLUMNS - 1], setup_recv.at[3])
            drain(ab_recv.at[0 : COLUMNS - 1], setup_send.at[3])
            rows = ab_recv[...].astype(F32)
            diagonal = iota((KPAD, KPAD), 0) == iota((KPAD, KPAD), 1)
            for b in range(BANDS):
                mine_b = rows[:, b * SLOTS : (b + 1) * SLOTS, :].reshape(COLUMNS * SLOTS, VIEW)
                column = jnp.sum(
                    jnp.where(diagonal, scalep[b : b + 1, :], 0.0), axis=1, keepdims=True
                )
                abk[b] = mm_tn(ohslot[...], mine_b.astype(BF16)) * column
        gained = prod[0] * abk[0, 0:VIEWS]
        for b in range(1, BANDS):
            gained = gained + prod[b] * abk[b, 0:VIEWS]
        up, down = halves(
            jnp.concatenate([gained, jnp.zeros((KPAD - VIEWS, VIEW), F32)], axis=0)
        )
        g_send[...] = (mm(ohslot[...], up) + mm(ohslot[...], down)).reshape(COLUMNS, SLOTS, VIEW)

        def send_rows(i):
            p = jnp.bitwise_xor(c, i)
            push(g_send.at[p], g_recv.at[it, c], g_ssem.at[it], g_rsem.at[it], (r, p))

        column_peers(send_rows)
        g_recv[it, pl.ds(c, 1)] = g_send[pl.ds(c, 1)]
        if it == 0:
            cond_load.wait()
        conducted = conduct(it)
        drain(g_recv.at[it, 0 : COLUMNS - 1], g_rsem.at[it])
        drain(g_recv.at[it, 0 : COLUMNS - 1], g_ssem.at[it])
        up, down = halves(g_recv[it].reshape(COLUMNS * SLOTS, VIEW))
        flux = mm(ohrow, up) + mm(ohrow, down) - emf[...] * patchq[mine, :]
        flux_out[...] = flux
        up, down = halves(flux)
        up, down = up.astype(F32), down.astype(F32)
        packed = jnp.zeros((PEERS, 2 * CAP), F32)
        for first_row in range(0, RB, 8):
            left, right = [], []
            for u in range(first_row, first_row + 8):
                rank = jnp.bitwise_and(code_mine[u : u + 1, :], CAP - 1)
                spread = jnp.where(
                    slot_rank == rank, jnp.where(slot_low, up[u : u + 1], down[u : u + 1]), 0.0
                )
                left.append(ohd[r * RB + u])
                right.append(spread.astype(BF16))
            packed = packed + mm_nt(jnp.concatenate(left, axis=1), jnp.concatenate(right, axis=1))
        f_send[:, 0, :] = packed

        def send_flux(i):
            p, where = peer(i)
            push(f_send.at[p], f_recv.at[it, me], f_ssem.at[it], f_rsem.at[it], where)

        all_peers(send_flux)
        f_recv[it, pl.ds(me, 1)] = f_send[pl.ds(me, 1)]
        if it == 0:
            weight = jnp.zeros((TILES, TILE), F32)
            for j in range(0, COLUMNS, 8):
                left, right = [], []
                for n in range(j, j + 8):
                    hit = tile_row == hi4[n : n + 1, :]
                    left.append(jnp.where(hit, em4[n : n + 1, :], 0.0).astype(BF16))
                    right.append(ohlo[n])
                weight = weight + mm_nt(
                    jnp.concatenate(left, axis=1), jnp.concatenate(right, axis=1)
                )
            esum[...] = weight
            lax.fori_loop(LATE, VIEWS, turn, 0, unroll=4)
        drain(f_recv.at[it, 0 : PEERS - 1], f_rsem.at[it])
        drain(f_recv.at[it, 0 : PEERS - 1], f_ssem.at[it])
        came = f_recv[it, :, 0, :]
        fh4[...] = rows_to_slots(came, False)
        fl4[...] = rows_to_slots(came, True)

        heat = jnp.zeros((2 * TILES, TILE), F32)
        for j in range(0, COLUMNS, 8):
            left, right = [], []
            for n in range(j, j + 8):
                hit = tile_row == hi4[n : n + 1, :]
                up = jnp.where(hit, fh4[n : n + 1, :], 0.0).astype(BF16)
                down = jnp.where(hit, fl4[n : n + 1, :], 0.0).astype(BF16)
                left.append(jnp.concatenate([up, down], axis=0))
                right.append(ohlo[n])
            heat = heat + mm_nt(jnp.concatenate(left, axis=1), jnp.concatenate(right, axis=1))
        old = temps[...]
        residual = (
            diag_ref[...] * old - conducted - (heat[0:TILES] + heat[TILES:]) - source_ref[...]
        )
        magnitude = jnp.abs(old)
        new = old - residual / (
            diag_ref[...] + 4.0 * magnitude * magnitude * magnitude * esum[...]
        )
        if it + 1 < ITERS:
            temps[...] = new
            send_halo(it + 1)
        else:
            node_out[...] = new


def shards(
    node_temp,
    node_diag,
    node_source,
    cond_blocks,
    cond_rows,
    cond_cols,
    view_blocks,
    view_scales,
    view_rows,
    view_cols,
    band_frac,
    absorb,
    emis,
    patch_dest,
    patch_node,
):
    vmem = pl.BlockSpec(memory_space=pltpu.VMEM)
    hbm = pl.BlockSpec(memory_space=pltpu.HBM)
    dma = pltpu.SemaphoreType.DMA
    node_final, patch_flux = pl.pallas_call(
        kernel,
        out_shape=(
            jax.ShapeDtypeStruct((TILES, TILE), F32),
            jax.ShapeDtypeStruct((RB, VIEW), F32),
        ),
        in_specs=[hbm] * 15,
        out_specs=(vmem, vmem),
        scratch_shapes=[
            pltpu.VMEM((RB, 1, VIEW), I32),
            pltpu.VMEM((RB, VIEW), I32),
            pltpu.VMEM((RB, VIEW), BF16),
            pltpu.VMEM((TILES, TILE), F32),
            pltpu.VMEM((1, VIEWS), I32),
            pltpu.VMEM((1, VIEWS), I32),
            pltpu.VMEM((RB, BANDS, VIEW), BF16),
            pltpu.VMEM((1, CONDS), I32),
            pltpu.VMEM((1, CONDS), I32),
            pltpu.VMEM((BANDS, VIEWS), F32),
            pltpu.VMEM((RB, BANDS, VIEW), BF16),
            pltpu.VMEM((TILES, TILE), F32),
            pltpu.VMEM((TILES, TILE), F32),
            pltpu.VMEM((CONDS, TILE, TILE), BF16),
            pltpu.VMEM((VIEWS, VIEW, VIEW), BF16),
            pltpu.VMEM((GROUP, PEERS, VIEW), BF16),
            pltpu.VMEM((COLUMNS, TILE, VIEW), BF16),
            pltpu.VMEM((RB, VIEW), I32),
            pltpu.VMEM((GROUP, VIEW), I32),
            pltpu.VMEM((BANDS, RB, VIEW), BF16),
            pltpu.VMEM((BANDS, GROUP, VIEW), BF16),
            pltpu.VMEM((PEERS, 2, 2 * CAP), F32),
            pltpu.VMEM((PEERS, 2, 2 * CAP), F32),
            pltpu.VMEM((COLUMNS, 1, REGIONS * CAP), F32),
            pltpu.VMEM((ITERS, PEERS, 1, REGIONS * CAP), F32),
            pltpu.VMEM((COLUMNS, BANDS * SLOTS, VIEW), BF16),
            pltpu.VMEM((COLUMNS, BANDS * SLOTS, VIEW), BF16),
            pltpu.VMEM((COLUMNS, SLOTS, VIEW), F32),
            pltpu.VMEM((ITERS, COLUMNS, SLOTS, VIEW), F32),
            pltpu.VMEM((PEERS, 1, 2 * CAP), F32),
            pltpu.VMEM((ITERS, PEERS, 1, 2 * CAP), F32),
            pltpu.VMEM((ITERS, 2, 1, TILE), F32),
            pltpu.VMEM((ITERS, 2, 1, TILE), F32),
            pltpu.VMEM((RB, VIEW), F32),
            pltpu.VMEM((COLUMNS, REGIONS * CAP), I32),
            pltpu.VMEM((COLUMNS, REGIONS * CAP), I32),
            pltpu.VMEM((COLUMNS, REGIONS * CAP), F32),
            pltpu.VMEM((COLUMNS, REGIONS * CAP), F32),
            pltpu.VMEM((COLUMNS, REGIONS * CAP), F32),
            pltpu.VMEM((GROUP, VIEW), F32),
            pltpu.VMEM((REGIONS, 2 * CAP, PEERS), BF16),
            pltpu.VMEM((BANDS, KPAD, VIEW), F32),
            pltpu.VMEM((BANDS, VIEWS, VIEW), F32),
            pltpu.VMEM((BANDS, KPAD, VIEW), F32),
            pltpu.VMEM((COLUMNS * SLOTS, KPAD), BF16),
            pltpu.VMEM((CPAD, 2 * TILE), F32),
            pltpu.VMEM((CPAD, TILE), F32),
            pltpu.VMEM((TILES, TILE), F32),
            pltpu.VMEM((8, CPAD), I32),
            pltpu.VMEM((8, KPAD), F32),
            dma((2,)),
            dma((13,)),
            dma((4,)),
            dma((4,)),
            dma((ITERS,)),
            dma((ITERS,)),
            dma((ITERS,)),
            dma((ITERS,)),
            dma((ITERS,)),
            dma((ITERS,)),
            dma((ITERS, 2)),
            dma((ITERS, 2)),
        ],
        compiler_params=pltpu.CompilerParams(
            collective_id=0, has_side_effects=True, vmem_limit_bytes=64 * 1024 * 1024
        ),
    )(
        patch_dest.reshape(RB, 1, VIEW),
        patch_node,
        emis,
        node_temp.reshape(TILES, TILE),
        view_rows.reshape(1, VIEWS),
        view_cols.reshape(1, VIEWS),
        band_frac,
        cond_rows.reshape(1, CONDS),
        cond_cols.reshape(1, CONDS),
        view_scales.reshape(VIEWS, BANDS).T,
        absorb,
        node_diag.reshape(TILES, TILE),
        node_source.reshape(TILES, TILE),
        cond_blocks.reshape(CONDS, TILE, TILE),
        view_blocks.reshape(VIEWS, VIEW, VIEW),
    )
    return node_final.reshape(TILES * TILE), patch_flux


def solution(mesh):
    placed = (
        P(("region", "blk")),
        P(("region", "blk")),
        P(("region", "blk")),
        P("region", "blk", None, None, None),
        P("region", "blk", None),
        P("region", "blk", None),
        P("region", "blk", None, None, None),
        P("region", "blk", None, None),
        P("region", "blk", None),
        P("region", "blk", None),
        P(("region", "blk"), None, None),
        P(("region", "blk"), None, None),
        P(("region", "blk"), None),
        P(("region", "blk"), None, None),
        P(("region", "blk"), None),
    )
    return jax.shard_map(
        shards,
        mesh=mesh,
        in_specs=placed,
        out_specs=(P(("region", "blk")), P(("region", "blk"), None)),
        check_vma=False,
    )
```

```python
import functools

import jax
import jax.numpy as jnp
from jax import lax
from jax.experimental import pallas as pl
from jax.experimental.pallas import tpu as pltpu
from jax.sharding import PartitionSpec as P

ITERS = 2
REGIONS = 4
COLUMNS = 32
PEERS = REGIONS * COLUMNS
BANDS = 4
RB = 16
VIEW = 256
VIEWS = 96
KPAD = 128
GROUP = RB * REGIONS
SLOTS = 8
CAP = 64
TILES = 64
TILE = 128
CONDS = 192
CPAD = 256
TURNED = 56
LATE = 72
MESH = pl.DeviceIdType.MESH
F32 = jnp.float32
BF16 = jnp.bfloat16
I32 = jnp.int32


FAR_GROUPS = [
    rx * 32 + z * 8
    for rx, z in sorted(
        ((rx, z) for rx in range(4) for z in range(4)),
        key=lambda g: -((0, 1, 2, 1)[g[0]] + (0, 1, 2, 1)[g[1]]),
    )
]


def mm(a, b):
    return jnp.dot(a, b, preferred_element_type=F32)


def mm_nt(a, b):
    return lax.dot_general(a, b, (((1,), (1,)), ((), ())), preferred_element_type=F32)


def mm_tn(a, b):
    return lax.dot_general(a, b, (((0,), (0,)), ((), ())), preferred_element_type=F32)


def iota(shape, dim):
    return lax.broadcasted_iota(I32, shape, dim)


def pick(mask):
    return jnp.where(mask, 1.0, 0.0).astype(BF16)


def halves(x):
    upper = x.astype(BF16)
    return upper, (x - upper.astype(F32)).astype(BF16)


def rows_to_slots(left, swap):
    low = iota((COLUMNS, 128), 1) < CAP
    part = [left[i * COLUMNS : (i + 1) * COLUMNS] for i in range(REGIONS)]
    pairs = []
    for i in range(0, REGIONS, 2):
        first, second = part[i], part[i + 1]
        if swap:
            first = pltpu.roll(first, CAP, 1)
        else:
            second = pltpu.roll(second, CAP, 1)
        pairs.append(jnp.where(low, first, second))
    return jnp.concatenate(pairs, axis=1)


def kernel(
    dest_hbm,
    node_hbm,
    emis_hbm,
    temp_hbm,
    vrow_hbm,
    vcol_hbm,
    frac_hbm,
    crow_hbm,
    ccol_hbm,
    scale_hbm,
    absorb_hbm,
    diag_hbm,
    source_hbm,
    cond_hbm,
    view_hbm,
    node_out,
    flux_out,
    dest_ref,
    node_ref,
    emis_ref,
    temps,
    vrow_ref,
    vcol_ref,
    frac_ref,
    crow_ref,
    ccol_ref,
    scale_ref,
    absorb_ref,
    diag_ref,
    source_ref,
    cb,
    vb,
    ohd,
    ohlo,
    code_mine,
    code_all,
    frac_mine,
    frac_all,
    req_send,
    req_recv,
    ans_send,
    ans_recv,
    ab_send,
    ab_recv,
    g_send,
    g_recv,
    f_send,
    f_recv,
    halo_send,
    halo_recv,
    emf,
    hi4,
    lo4,
    em4,
    fh4,
    fl4,
    patchq,
    ftl,
    ecol,
    prod,
    abk,
    ohslot,
    colt,
    terms,
    esum,
    pads,
    scalep,
    load_sem,
    small_sem,
    setup_send,
    setup_recv,
    ans_ssem,
    ans_rsem,
    g_ssem,
    g_rsem,
    f_ssem,
    f_rsem,
    halo_ssem,
    halo_rsem,
):
    r = lax.axis_index("region")
    c = lax.axis_index("blk")
    me = r * COLUMNS + c

    def peer(i):
        p = jnp.bitwise_xor(me, i)
        return p, (lax.shift_right_logical(p, 5), jnp.bitwise_and(p, COLUMNS - 1))

    def all_peers(step):
        for base in FAR_GROUPS:
            if base:
                lax.fori_loop(0, 8, lambda w, z: (step(base + jnp.bitwise_xor(w, 4)), z)[1], 0)
            else:
                for w in (0, 1, 2, 3, 5, 6, 7):
                    step(w ^ 4)

    def column_peers(step):
        far = 20
        lax.fori_loop(0, far, lambda w, z: (step(jnp.bitwise_xor(w, far)), z)[1], 0)
        lax.fori_loop(far + 1, COLUMNS, lambda w, z: (step(jnp.bitwise_xor(w, far)), z)[1], 0)

    def push(src, dst, ssem, rsem, where):
        pltpu.make_async_remote_copy(
            src_ref=src,
            dst_ref=dst,
            send_sem=ssem,
            recv_sem=rsem,
            device_id=where,
            device_id_type=MESH,
        ).start()

    def drain(ref, sem):
        pltpu.make_async_copy(ref, ref, sem).wait()

    barrier = pltpu.get_barrier_semaphore()

    def greet(i):
        pl.semaphore_signal(barrier, inc=1, device_id=peer(i)[1], device_id_type=MESH)

    all_peers(greet)

    cond_load = pltpu.make_async_copy(cond_hbm, cb, load_sem.at[0])
    view_load = pltpu.make_async_copy(view_hbm, vb, load_sem.at[1])
    pairs = [
        (dest_hbm, dest_ref),
        (node_hbm, node_ref),
        (emis_hbm, emis_ref),
        (temp_hbm, temps),
        (vrow_hbm, vrow_ref),
        (vcol_hbm, vcol_ref),
        (frac_hbm, frac_ref),
        (crow_hbm, crow_ref),
        (ccol_hbm, ccol_ref),
        (scale_hbm, scale_ref),
        (absorb_hbm, absorb_ref),
        (diag_hbm, diag_ref),
        (source_hbm, source_ref),
    ]
    small = [
        pltpu.make_async_copy(src, dst, small_sem.at[n]) for n, (src, dst) in enumerate(pairs)
    ]
    for load in small:
        load.start()
    cond_load.start()
    view_load.start()

    for load in small:
        load.wait()

    emf[...] = emis_ref[...].astype(F32)
    upper_tri = pick(iota((VIEW, VIEW), 0) < iota((VIEW, VIEW), 1))
    peer_row = iota((PEERS, VIEW), 0)
    slot_row = iota((2 * CAP, VIEW), 0)
    slot_rank = jnp.bitwise_and(slot_row, CAP - 1)
    slot_low = slot_row < CAP

    def route(u, carry):
        count, first, second = carry
        dest = dest_ref[u]
        node = node_ref[pl.ds(u, 1), :]
        hit = jnp.where(peer_row == dest, 1.0, 0.0)
        hit16 = hit.astype(BF16)
        before = mm(hit16, upper_tri)
        rank = jnp.sum(hit * (before + count), axis=0, keepdims=True).astype(I32)
        code_mine[pl.ds(u, 1), :] = dest * CAP + rank
        ohd[r * RB + u] = hit16
        high = (lax.shift_right_logical(node, 7) + 1).astype(F32)
        low = jnp.bitwise_and(node, TILE - 1).astype(F32)
        match = slot_rank == rank
        one = jnp.where(match, jnp.where(slot_low, high, emf[pl.ds(u, 1), :]), 0.0)
        two = jnp.where(match & slot_low, low, 0.0)
        first = first + mm_nt(hit16, one.astype(BF16))
        second = second + mm_nt(hit16, two.astype(BF16))
        count = count + hit[:, VIEW - 1 :] + before[:, VIEW - 1 :]
        return count, first, second

    zero_rows = jnp.zeros((PEERS, 2 * CAP), F32)
    _, first, second = lax.fori_loop(
        0, RB, route, (jnp.zeros((PEERS, 1), F32), zero_rows, zero_rows), unroll=2
    )
    lane_low = iota((PEERS, 2 * CAP), 1) < CAP
    req_send[:, 0, :] = first * jnp.where(lane_low, 128.0, 1.0) + second
    req_send[:, 1, :] = zero_rows

    pads[...] = jnp.full((8, CPAD), -1, I32)
    pads[0:1, 0:VIEWS] = vrow_ref[...]
    pads[1:2, 0:VIEWS] = vcol_ref[...]
    pads[2:3, 0:CONDS] = crow_ref[...]
    pads[3:4, 0:CONDS] = ccol_ref[...]
    vrow = pads[0:1, 0:KPAD]
    vcol = pads[1:2, 0:KPAD]
    crow = pads[2:3, :]
    ccol = pads[3:4, :]
    owner = lax.shift_right_arithmetic(vrow, 4)
    offset = jnp.bitwise_and(vrow, RB - 1)
    owner_hit = pick(iota((COLUMNS, KPAD), 0) == owner)
    offset_hit = jnp.where(iota((128, KPAD), 0) == offset, 1.0, 0.0)
    present = jnp.where(mm_nt(owner_hit, offset_hit.astype(BF16)) > 0.5, 1.0, 0.0)
    tri128 = pick(iota((128, 128), 0) < iota((128, 128), 1))
    place = mm(present.astype(BF16), tri128)
    place_of = mm_tn(place.astype(BF16), owner_hit)
    slot = owner * SLOTS + jnp.sum(offset_hit * place_of, axis=0, keepdims=True).astype(I32)
    ohslot[...] = pick(iota((COLUMNS * SLOTS, KPAD), 0) == slot)
    slot_lane = iota((COLUMNS, 128), 1)
    lane_slot = jnp.bitwise_and(slot_lane, SLOTS - 1).astype(F32)
    table = jnp.zeros((COLUMNS, 128), F32)
    for f in range(RB):
        held = jnp.where(present[:, f : f + 1] > 0.5, place[:, f : f + 1], -1.0)
        table = table + jnp.where(lane_slot == held, f + 1.0, 0.0)
    own_lanes = lax.shift_right_logical(slot_lane, 3) == jnp.bitwise_and(c, 15)
    req_send[pl.ds(r * COLUMNS, COLUMNS), 1, :] = jnp.where(own_lanes, table, 0.0)

    for b in range(BANDS):
        frac_mine[b] = frac_ref[:, b, :]
    ohcol = jnp.where(iota((KPAD, KPAD), 0) == vcol, 1.0, 0.0).T[:, 0:GROUP].astype(BF16)
    scalep[...] = jnp.zeros((8, KPAD), F32)
    scalep[0:BANDS, 0:VIEWS] = scale_ref[...]
    terms[...] = jnp.zeros((CPAD, TILE), F32)
    oh_ctile = pick(iota((TILES, CPAD), 0) == crow)
    ccol_at = jnp.where(ccol == 0, TILES, jnp.where(ccol == TILES + 1, TILES + 1, ccol - 1))
    oh_ccol = pick(iota((TILES + 16, CPAD), 0) == jnp.where(ccol < 0, -1, ccol_at))

    pl.semaphore_wait(barrier, PEERS - 1)

    mine = pl.ds(pl.multiple_of(r * RB, RB), RB)
    def send_request(i):
        p, where = peer(i)
        push(req_send.at[p], req_recv.at[me], setup_send.at[0], setup_recv.at[0], where)

    all_peers(send_request)
    for i in range(1, REGIONS):
        where = (jnp.bitwise_xor(r, i), c)
        push(code_mine, code_all.at[mine], setup_send.at[1], setup_recv.at[1], where)
    req_recv[pl.ds(me, 1)] = req_send[pl.ds(me, 1)]
    code_all[mine, :] = code_mine[...]
    frac_all[:, mine, :] = frac_mine[...]

    after = lax.rem(me + 1, PEERS)
    ahead = lax.rem(me + PEERS - 1, PEERS)
    after_id = (lax.shift_right_logical(after, 5), jnp.bitwise_and(after, COLUMNS - 1))
    ahead_id = (lax.shift_right_logical(ahead, 5), jnp.bitwise_and(ahead, COLUMNS - 1))

    def send_halo(it):
        halo_send[it, 0] = temps[TILES - 1 :, :]
        halo_send[it, 1] = temps[0:1, :]
        push(
            halo_send.at[it, 0], halo_recv.at[it, 0], halo_ssem.at[it, 0], halo_rsem.at[it, 0], after_id
        )
        push(
            halo_send.at[it, 1], halo_recv.at[it, 1], halo_ssem.at[it, 1], halo_rsem.at[it, 1], ahead_id
        )

    def wait_halo(it):
        for s in range(2):
            drain(halo_recv.at[it, s], halo_rsem.at[it, s])
            drain(halo_send.at[it, s], halo_ssem.at[it, s])

    send_halo(0)

    view_load.wait()

    def turn(k, carry):
        vb[k] = vb[k].T
        return carry

    lax.fori_loop(0, TURNED, turn, 0, unroll=4)
    drain(req_recv.at[0 : PEERS - 1], setup_recv.at[0])
    drain(req_recv.at[0 : PEERS - 1], setup_send.at[0])
    asked = req_recv[:, 0, :]
    code4 = rows_to_slots(asked, False).astype(I32)
    em4[...] = rows_to_slots(asked, True)
    hi4[...] = lax.shift_right_logical(code4, 7) - 1
    lo4[...] = jnp.bitwise_and(code4, TILE - 1)
    tile_row = iota((TILES, VIEW), 0)
    node_row = iota((TILE, VIEW), 0)

    def answer(it):
        up, down = halves(temps[...])
        both = jnp.concatenate([up, down], axis=0)

        def look(j, carry):
            if it == 0:
                hot = pick(node_row == lo4[pl.ds(j, 1), :])
                ohlo[j] = hot
            else:
                hot = ohlo[j]
            found = mm(both, hot)
            found = found[0:TILES] + found[TILES:]
            ans_send[j] = jnp.sum(
                jnp.where(tile_row == hi4[pl.ds(j, 1), :], found, 0.0), axis=0, keepdims=True
            )
            return carry

        lax.fori_loop(0, COLUMNS, look, 0, unroll=16)

        def send(i):
            where = peer(i)[1]
            push(ans_send.at[where[1]], ans_recv.at[it, me], ans_ssem.at[it], ans_rsem.at[it], where)

        all_peers(send)
        ans_recv[it, pl.ds(me, 1)] = ans_send[pl.ds(c, 1)]

    def conduct(it):
        wait_halo(it)
        before = jnp.where(me == 0, 0.0, halo_recv[it, 0])
        behind = jnp.where(me == PEERS - 1, 0.0, halo_recv[it, 1])
        edge_row = iota((16, TILE), 0)
        edges = jnp.where(edge_row == 0, before, jnp.where(edge_row == 1, behind, 0.0))
        up, down = halves(jnp.concatenate([temps[...], edges], axis=0))
        colt[...] = mm_tn(oh_ccol, jnp.concatenate([up, down], axis=1))
        eight = iota((8, TILE), 0)

        def group(g, carry):
            rows = colt[pl.ds(pl.multiple_of(g * 8, 8), 8), :]
            left = jnp.concatenate([rows[:, 0:TILE], rows[:, TILE:]], axis=0).astype(BF16)
            total = jnp.zeros((8, TILE), F32)
            for a in range(8):
                part = mm_nt(left, cb[g * 8 + a])
                total = jnp.where(eight == a, part[0:8] + part[8:16], total)
            terms[pl.ds(pl.multiple_of(g * 8, 8), 8), :] = total
            return carry

        lax.fori_loop(0, CONDS // 8, group, 0)
        up, down = halves(terms[...])
        return mm(oh_ctile, up) + mm(oh_ctile, down)

    answer(0)
    for i in range(1, REGIONS):
        where = (jnp.bitwise_xor(r, i), c)
        push(frac_mine, frac_all.at[:, mine, :], setup_send.at[2], setup_recv.at[2], where)
    others = pl.ds(0, (REGIONS - 1) * RB)
    drain(code_all.at[others], setup_recv.at[1])
    drain(code_all.at[others], setup_send.at[1])

    def build_dest(n, carry):
        q = lax.rem(n + (r + 1) * RB, GROUP)
        ohd[q] = pick(peer_row == lax.shift_right_logical(code_all[pl.ds(q, 1), :], 6))
        return carry

    lax.fori_loop(0, GROUP - RB, build_dest, 0, unroll=8)

    codes = req_recv[pl.ds(r * COLUMNS, COLUMNS), 1, :]
    row_codes = jnp.concatenate(
        [
            jnp.sum(codes[0:16], axis=0, keepdims=True),
            jnp.sum(codes[16:32], axis=0, keepdims=True),
        ],
        axis=1,
    ).astype(I32)
    ohrow = pick(iota((RB, COLUMNS * SLOTS), 0) + 1 == row_codes)
    for b in range(0, BANDS, 2):
        pair = [
            mm_tn(ohrow, absorb_ref[:, b + i, :]).reshape(COLUMNS, SLOTS, VIEW) for i in range(2)
        ]
        ab_send[:, b * SLOTS : (b + 2) * SLOTS, :] = jnp.concatenate(pair, axis=1).astype(BF16)

    def send_absorb(i):
        p = jnp.bitwise_xor(c, i)
        push(ab_send.at[p], ab_recv.at[c], setup_send.at[3], setup_recv.at[3], (r, p))

    column_peers(send_absorb)
    ab_recv[pl.ds(c, 1)] = ab_send[pl.ds(c, 1)]
    lax.fori_loop(TURNED, LATE, turn, 0, unroll=4)
    drain(frac_all.at[:, others, :], setup_recv.at[2])
    drain(frac_all.at[:, others, :], setup_send.at[2])
    rank_row = iota((CAP, VIEW), 0)

    for it in range(ITERS):
        if it > 0:
            answer(it)
        drain(ans_recv.at[it, 0 : PEERS - 1], ans_rsem.at[it])
        drain(ans_recv.at[it, 0 : PEERS - 1], ans_ssem.at[it])
        up, down = halves(ans_recv[it, :, 0, :].T)
        for i in range(REGIONS):
            span = slice(i * CAP, (i + 1) * CAP)
            ftl[i] = jnp.concatenate([up[span], down[span]], axis=0)

        def unpack(q, carry):
            found = mm(ftl[lax.shift_right_logical(q, 4)], ohd[q])
            found = found[0:CAP] + found[CAP:]
            rank = jnp.bitwise_and(code_all[pl.ds(q, 1), :], CAP - 1)
            value = jnp.sum(jnp.where(rank_row == rank, found, 0.0), axis=0, keepdims=True)
            squared = value * value
            patchq[pl.ds(q, 1), :] = squared * squared
            return carry

        lax.fori_loop(0, GROUP, unpack, 0, unroll=32)
        quartic = patchq[...]
        for b in range(BANDS):
            emit = (frac_all[b].astype(F32) * quartic).astype(BF16)
            ecol[b] = mm(ohcol, emit)
        def view(k, carry):
            prod[:, k, :] = mm(ecol[:, k, :].astype(BF16), vb[k])
            return carry

        def view_unturned(k, carry):
            prod[:, k, :] = mm_nt(ecol[:, k, :].astype(BF16), vb[k])
            return carry

        if it == 0:
            lax.fori_loop(0, LATE, view, 0, unroll=36)
            lax.fori_loop(LATE, VIEWS, view_unturned, 0, unroll=24)
        else:
            lax.fori_loop(0, VIEWS, view, 0, unroll=32)
        if it == 0:
            drain(ab_recv.at[0 : COLUMNS - 1], setup_recv.at[3])
            drain(ab_recv.at[0 : COLUMNS - 1], setup_send.at[3])
            rows = ab_recv[...].astype(F32)
            diagonal = iota((KPAD, KPAD), 0) == iota((KPAD, KPAD), 1)
            for b in range(BANDS):
                mine_b = rows[:, b * SLOTS : (b + 1) * SLOTS, :].reshape(COLUMNS * SLOTS, VIEW)
                column = jnp.sum(
                    jnp.where(diagonal, scalep[b : b + 1, :], 0.0), axis=1, keepdims=True
                )
                abk[b] = mm_tn(ohslot[...], mine_b.astype(BF16)) * column
        gained = prod[0] * abk[0, 0:VIEWS]
        for b in range(1, BANDS):
            gained = gained + prod[b] * abk[b, 0:VIEWS]
        up, down = halves(
            jnp.concatenate([gained, jnp.zeros((KPAD - VIEWS, VIEW), F32)], axis=0)
        )
        g_send[...] = (mm(ohslot[...], up) + mm(ohslot[...], down)).reshape(COLUMNS, SLOTS, VIEW)

        def send_rows(i):
            p = jnp.bitwise_xor(c, i)
            push(g_send.at[p], g_recv.at[it, c], g_ssem.at[it], g_rsem.at[it], (r, p))

        column_peers(send_rows)
        g_recv[it, pl.ds(c, 1)] = g_send[pl.ds(c, 1)]
        if it == 0:
            cond_load.wait()
        conducted = conduct(it)
        drain(g_recv.at[it, 0 : COLUMNS - 1], g_rsem.at[it])
        drain(g_recv.at[it, 0 : COLUMNS - 1], g_ssem.at[it])
        up, down = halves(g_recv[it].reshape(COLUMNS * SLOTS, VIEW))
        flux = mm(ohrow, up) + mm(ohrow, down) - emf[...] * patchq[mine, :]
        flux_out[...] = flux
        up, down = halves(flux)
        up, down = up.astype(F32), down.astype(F32)
        packed = jnp.zeros((PEERS, 2 * CAP), F32)
        for first_row in range(0, RB, 8):
            left, right = [], []
            for u in range(first_row, first_row + 8):
                rank = jnp.bitwise_and(code_mine[u : u + 1, :], CAP - 1)
                spread = jnp.where(
                    slot_rank == rank, jnp.where(slot_low, up[u : u + 1], down[u : u + 1]), 0.0
                )
                left.append(ohd[r * RB + u])
                right.append(spread.astype(BF16))
            packed = packed + mm_nt(jnp.concatenate(left, axis=1), jnp.concatenate(right, axis=1))
        f_send[:, 0, :] = packed

        def send_flux(i):
            p, where = peer(i)
            push(f_send.at[p], f_recv.at[it, me], f_ssem.at[it], f_rsem.at[it], where)

        all_peers(send_flux)
        f_recv[it, pl.ds(me, 1)] = f_send[pl.ds(me, 1)]
        if it == 0:
            weight = jnp.zeros((TILES, TILE), F32)
            for j in range(0, COLUMNS, 8):
                left, right = [], []
                for n in range(j, j + 8):
                    hit = tile_row == hi4[n : n + 1, :]
                    left.append(jnp.where(hit, em4[n : n + 1, :], 0.0).astype(BF16))
                    right.append(ohlo[n])
                weight = weight + mm_nt(
                    jnp.concatenate(left, axis=1), jnp.concatenate(right, axis=1)
                )
            esum[...] = weight
            lax.fori_loop(LATE, VIEWS, turn, 0, unroll=4)
        drain(f_recv.at[it, 0 : PEERS - 1], f_rsem.at[it])
        drain(f_recv.at[it, 0 : PEERS - 1], f_ssem.at[it])
        came = f_recv[it, :, 0, :]
        fh4[...] = rows_to_slots(came, False)
        fl4[...] = rows_to_slots(came, True)

        heat = jnp.zeros((2 * TILES, TILE), F32)
        for j in range(0, COLUMNS, 8):
            left, right = [], []
            for n in range(j, j + 8):
                hit = tile_row == hi4[n : n + 1, :]
                up = jnp.where(hit, fh4[n : n + 1, :], 0.0).astype(BF16)
                down = jnp.where(hit, fl4[n : n + 1, :], 0.0).astype(BF16)
                left.append(jnp.concatenate([up, down], axis=0))
                right.append(ohlo[n])
            heat = heat + mm_nt(jnp.concatenate(left, axis=1), jnp.concatenate(right, axis=1))
        old = temps[...]
        residual = (
            diag_ref[...] * old - conducted - (heat[0:TILES] + heat[TILES:]) - source_ref[...]
        )
        magnitude = jnp.abs(old)
        new = old - residual / (
            diag_ref[...] + 4.0 * magnitude * magnitude * magnitude * esum[...]
        )
        if it + 1 < ITERS:
            temps[...] = new
            send_halo(it + 1)
        else:
            node_out[...] = new


def shards(
    node_temp,
    node_diag,
    node_source,
    cond_blocks,
    cond_rows,
    cond_cols,
    view_blocks,
    view_scales,
    view_rows,
    view_cols,
    band_frac,
    absorb,
    emis,
    patch_dest,
    patch_node,
):
    vmem = pl.BlockSpec(memory_space=pltpu.VMEM)
    hbm = pl.BlockSpec(memory_space=pltpu.HBM)
    dma = pltpu.SemaphoreType.DMA
    node_final, patch_flux = pl.pallas_call(
        kernel,
        out_shape=(
            jax.ShapeDtypeStruct((TILES, TILE), F32),
            jax.ShapeDtypeStruct((RB, VIEW), F32),
        ),
        in_specs=[hbm] * 15,
        out_specs=(vmem, vmem),
        scratch_shapes=[
            pltpu.VMEM((RB, 1, VIEW), I32),
            pltpu.VMEM((RB, VIEW), I32),
            pltpu.VMEM((RB, VIEW), BF16),
            pltpu.VMEM((TILES, TILE), F32),
            pltpu.VMEM((1, VIEWS), I32),
            pltpu.VMEM((1, VIEWS), I32),
            pltpu.VMEM((RB, BANDS, VIEW), BF16),
            pltpu.VMEM((1, CONDS), I32),
            pltpu.VMEM((1, CONDS), I32),
            pltpu.VMEM((BANDS, VIEWS), F32),
            pltpu.VMEM((RB, BANDS, VIEW), BF16),
            pltpu.VMEM((TILES, TILE), F32),
            pltpu.VMEM((TILES, TILE), F32),
            pltpu.VMEM((CONDS, TILE, TILE), BF16),
            pltpu.VMEM((VIEWS, VIEW, VIEW), BF16),
            pltpu.VMEM((GROUP, PEERS, VIEW), BF16),
            pltpu.VMEM((COLUMNS, TILE, VIEW), BF16),
            pltpu.VMEM((RB, VIEW), I32),
            pltpu.VMEM((GROUP, VIEW), I32),
            pltpu.VMEM((BANDS, RB, VIEW), BF16),
            pltpu.VMEM((BANDS, GROUP, VIEW), BF16),
            pltpu.VMEM((PEERS, 2, 2 * CAP), F32),
            pltpu.VMEM((PEERS, 2, 2 * CAP), F32),
            pltpu.VMEM((COLUMNS, 1, REGIONS * CAP), F32),
            pltpu.VMEM((ITERS, PEERS, 1, REGIONS * CAP), F32),
            pltpu.VMEM((COLUMNS, BANDS * SLOTS, VIEW), BF16),
            pltpu.VMEM((COLUMNS, BANDS * SLOTS, VIEW), BF16),
            pltpu.VMEM((COLUMNS, SLOTS, VIEW), F32),
            pltpu.VMEM((ITERS, COLUMNS, SLOTS, VIEW), F32),
            pltpu.VMEM((PEERS, 1, 2 * CAP), F32),
            pltpu.VMEM((ITERS, PEERS, 1, 2 * CAP), F32),
            pltpu.VMEM((ITERS, 2, 1, TILE), F32),
            pltpu.VMEM((ITERS, 2, 1, TILE), F32),
            pltpu.VMEM((RB, VIEW), F32),
            pltpu.VMEM((COLUMNS, REGIONS * CAP), I32),
            pltpu.VMEM((COLUMNS, REGIONS * CAP), I32),
            pltpu.VMEM((COLUMNS, REGIONS * CAP), F32),
            pltpu.VMEM((COLUMNS, REGIONS * CAP), F32),
            pltpu.VMEM((COLUMNS, REGIONS * CAP), F32),
            pltpu.VMEM((GROUP, VIEW), F32),
            pltpu.VMEM((REGIONS, 2 * CAP, PEERS), BF16),
            pltpu.VMEM((BANDS, KPAD, VIEW), F32),
            pltpu.VMEM((BANDS, VIEWS, VIEW), F32),
            pltpu.VMEM((BANDS, KPAD, VIEW), F32),
            pltpu.VMEM((COLUMNS * SLOTS, KPAD), BF16),
            pltpu.VMEM((CPAD, 2 * TILE), F32),
            pltpu.VMEM((CPAD, TILE), F32),
            pltpu.VMEM((TILES, TILE), F32),
            pltpu.VMEM((8, CPAD), I32),
            pltpu.VMEM((8, KPAD), F32),
            dma((2,)),
            dma((13,)),
            dma((4,)),
            dma((4,)),
            dma((ITERS,)),
            dma((ITERS,)),
            dma((ITERS,)),
            dma((ITERS,)),
            dma((ITERS,)),
            dma((ITERS,)),
            dma((ITERS, 2)),
            dma((ITERS, 2)),
        ],
        compiler_params=pltpu.CompilerParams(
            collective_id=0, has_side_effects=True, vmem_limit_bytes=64 * 1024 * 1024
        ),
    )(
        patch_dest.reshape(RB, 1, VIEW),
        patch_node,
        emis,
        node_temp.reshape(TILES, TILE),
        view_rows.reshape(1, VIEWS),
        view_cols.reshape(1, VIEWS),
        band_frac,
        cond_rows.reshape(1, CONDS),
        cond_cols.reshape(1, CONDS),
        view_scales.reshape(VIEWS, BANDS).T,
        absorb,
        node_diag.reshape(TILES, TILE),
        node_source.reshape(TILES, TILE),
        cond_blocks.reshape(CONDS, TILE, TILE),
        view_blocks.reshape(VIEWS, VIEW, VIEW),
    )
    return node_final.reshape(TILES * TILE), patch_flux


def solution(mesh):
    placed = (
        P(("region", "blk")),
        P(("region", "blk")),
        P(("region", "blk")),
        P("region", "blk", None, None, None),
        P("region", "blk", None),
        P("region", "blk", None),
        P("region", "blk", None, None, None),
        P("region", "blk", None, None),
        P("region", "blk", None),
        P("region", "blk", None),
        P(("region", "blk"), None, None),
        P(("region", "blk"), None, None),
        P(("region", "blk"), None),
        P(("region", "blk"), None, None),
        P(("region", "blk"), None),
    )
    return jax.shard_map(
        shards,
        mesh=mesh,
        in_specs=placed,
        out_specs=(P(("region", "blk")), P(("region", "blk"), None)),
        check_vma=False,
    )
```
